256 devices in a mesh: seq: 32 (over y, z_hi, core), lat: 8 (over z_lo, x).
Axes of the slice: x: 4, y: 4, z: 8 (z_hi: 4, z_lo: 2; z = z_hi * 2 + z_lo), core: 2. Of those that a mesh axis runs over, the one named last changes fastest.
Arguments:
- q_raw: bfloat16 [12288, 2048], P('seq', 'lat'), may hold values from -6 to 6
- k_raw: bfloat16 [12288, 2048], P('seq', 'lat'), may hold values from -6 to 6
- v_raw: bfloat16 [12288, 4096], P('seq', 'lat'), may hold values from -6 to 6
- z_gate: bfloat16 [12288, 4096], P('seq', 'lat'), may hold values from -6 to 6
- beta_raw: float32 [32, 12288], P('lat', 'seq'), may hold values from -9 to 4
- decay_log: float32 [32, 12288], P('lat', 'seq'), may hold values from -1.1 to 0
- conv_q: float32 [4, 2048], P(None, 'lat'), may hold values from -3 to 3
- conv_k: float32 [4, 2048], P(None, 'lat'), may hold values from -3 to 3
- conv_v: float32 [4, 4096], P(None, 'lat'), may hold values from -3 to 3
- norm_gain: float32 [128], replicated, may hold values from 0.1 to 1.9
- w_out: bfloat16 [4096, 2048], P('lat'), may hold values from -0.125 to 0.125
- residual: bfloat16 [12288, 2048], P('seq', 'lat'), may hold values from -24 to 24
- post_gain: float32 [2048], replicated, may hold values from 0.1 to 1.9
- w_enc: bfloat16 [2048, 16384], P('seq', 'lat'), may hold values from -0.125 to 0.125
- b_enc: float32 [16384], P('lat'), may hold values from -4 to 4
- w_dec: bfloat16 [2048, 16384], P('seq', 'lat'), may hold values from -0.09375 to 0.09375
- b_dec: float32 [2048], P('lat'), may hold values from -2 to 2
Outputs:
- layer_out: bfloat16 [12288, 2048], P('seq', 'lat')
The draws below stay inside these ranges and needn't reach their ends.
All inputs are finite; a program needn't handle non-finite values.
Results may differ from the reference program's by a relative error of at most 0.006.
Values may be sent and summed in bfloat16 or wider, within the bound.
A program may use at most 128 MiB of HBM per device.

```python
import jax
import jax.numpy as jnp
from jax import lax

D = 2048
HK = 16
VALUE_HEADS = 32
DK = 128
VALUE_HEAD_WIDTH = 128
CONV = 4
SPAN = 64
LATENTS = 16384
TOK_DEV = 384
SEQUENCE_TOKENS = 12288


def draw_beta_raw(key, part):
    key = jax.random.fold_in(key, 7)
    random_subkeys = jax.random.split(key, 2)
    center = jax.random.uniform(random_subkeys[0], (VALUE_HEADS, 1), minval=-5.0, maxval=0.5)
    jitter = jax.random.normal(random_subkeys[1], (VALUE_HEADS, SEQUENCE_TOKENS))
    return jnp.clip(center + jitter, -9.0, 4.0).astype(jnp.float32)


def draw_decay_log(key, part):
    key = jax.random.fold_in(key, 11)
    random_subkeys = jax.random.split(key, 7)
    slow_share = 0.5
    slow = jax.random.uniform(random_subkeys[0], (VALUE_HEADS, 1, 1)) < slow_share
    fast_rate = jax.random.uniform(random_subkeys[1], (VALUE_HEADS, 1, 1), minval=0.045, maxval=0.08)
    slow_rate = jax.random.uniform(random_subkeys[2], (VALUE_HEADS, 1, 1), minval=0.05, maxval=0.3) / SEQUENCE_TOKENS
    base_rate = jnp.where(slow, slow_rate, fast_rate)
    block_count = SEQUENCE_TOKENS // TOK_DEV
    device_factor = jnp.exp(jax.random.uniform(random_subkeys[3], (VALUE_HEADS, block_count, 1), minval=-0.7, maxval=0.7))
    rough = jnp.exp(jax.random.uniform(random_subkeys[4], (VALUE_HEADS, block_count, TOK_DEV), minval=-0.7, maxval=0.7))
    decay_speed = (base_rate * device_factor * rough).reshape(VALUE_HEADS, SEQUENCE_TOKENS)
    sudden_spike = jax.random.uniform(random_subkeys[5], (VALUE_HEADS, SEQUENCE_TOKENS)) < 3.0 / SEQUENCE_TOKENS
    sharp_decline = jnp.log(1.0 - jax.random.uniform(random_subkeys[6], (VALUE_HEADS, SEQUENCE_TOKENS), minval=0.2, maxval=0.5))
    return jnp.clip(jnp.where(sudden_spike, sharp_decline, 0.0) - decay_speed, -1.1, 0.0).astype(jnp.float32)


def draw_residual(key, part):
    key = jax.random.fold_in(key, 5)
    random_subkeys = jax.random.split(key, 3)
    row_scale = jnp.exp(jax.random.uniform(random_subkeys[0], (SEQUENCE_TOKENS, 1), minval=-1.2, maxval=1.1))
    col_scale = jnp.exp(jax.random.uniform(random_subkeys[1], (1, D), minval=-1.2, maxval=1.1))
    base = jax.random.normal(random_subkeys[2], (SEQUENCE_TOKENS, D))
    return jnp.clip(base * row_scale * col_scale, -24.0, 24.0).astype(jnp.bfloat16)


def with_spikes(array, stream_key, source, target, blocks, factor):
    def block_of(dim):
        return (jnp.arange(array.shape[dim]) // (array.shape[dim] // blocks)).reshape((-1,) + (1,) * (array.ndim - 1 - dim))

    first = jax.random.permutation(stream_key, blocks)[block_of(target)]
    second = (block_of(target) + blocks // 2) % blocks
    return jnp.where((block_of(source) == first) | (block_of(source) == second), factor * array, array)


def steps_of(stream_key, shape, cuts, low, top_value):
    level = 1.0
    for dim, parts in cuts:
        steps = jax.random.uniform(jax.random.fold_in(jax.random.fold_in(stream_key, 6), dim), (parts,), jnp.float32, low / len(cuts), top_value / len(cuts))
        level = level * jnp.repeat(jnp.exp(steps), shape[dim] // parts).reshape((-1,) + (1,) * (len(shape) - 1 - dim))
    return level


def normal_values(stream_key, dims, width, bound, shards=(), kind=jnp.bfloat16):
    drawn = jax.random.normal(stream_key, dims, jnp.float32) * width
    if len(shards) > 0:
        drawn = steps_of(stream_key, dims, shards, -0.22, 0.18) * drawn
    return jnp.clip(drawn, min=-bound, max=bound).astype(kind)


def bell_draw_with(stream_key, shape, deviation, bound, pieces, heavy, kind=jnp.bfloat16):
    drawn = deviation * jax.random.normal(stream_key, shape, jnp.float32)
    if pieces:
        drawn = drawn * steps_of(stream_key, shape, pieces, -0.22, 0.18)
    return jnp.clip(with_spikes(drawn, jax.random.fold_in(stream_key, 3), *heavy), -bound, bound).astype(kind)


def setup_inputs(seed: int = 0) -> dict:
    streams_of = jax.random.split(jax.random.key(seed), 18)
    return {
        "q_raw": normal_values(streams_of[0], (SEQUENCE_TOKENS, HK * DK), 1.0, 6.0, ((0, 32), (1, 8))),
        "k_raw": normal_values(streams_of[1], (SEQUENCE_TOKENS, HK * DK), 1.0, 6.0, ((0, 32), (1, 8))),
        "v_raw": normal_values(streams_of[2], (SEQUENCE_TOKENS, VALUE_HEADS * VALUE_HEAD_WIDTH), 1.0, 6.0, ((0, 32), (1, 8))),
        "z_gate": normal_values(streams_of[3], (SEQUENCE_TOKENS, VALUE_HEADS * VALUE_HEAD_WIDTH), 1.0, 6.0, ((0, 32), (1, 8))),
        "beta_raw": draw_beta_raw(jax.random.fold_in(streams_of[17], 71), 0),
        "decay_log": draw_decay_log(jax.random.fold_in(streams_of[17], 71), 0),
        "conv_q": normal_values(streams_of[6], (CONV, HK * DK), 0.5, 3.0, ((1, 8),), jnp.float32),
        "conv_k": normal_values(streams_of[7], (CONV, HK * DK), 0.5, 3.0, ((1, 8),), jnp.float32),
        "conv_v": normal_values(streams_of[8], (CONV, VALUE_HEADS * VALUE_HEAD_WIDTH), 0.5, 3.0, ((1, 8),), jnp.float32),
        "norm_gain": jnp.clip(1.0 + 0.18 * jax.random.normal(streams_of[9], (VALUE_HEAD_WIDTH,), jnp.float32), 0.1, 1.9),
        "w_out": bell_draw_with(streams_of[10], (VALUE_HEADS * VALUE_HEAD_WIDTH, D), (VALUE_HEADS * VALUE_HEAD_WIDTH) ** -0.5, 0.125, ((0, 8),), (0, 1, 8, 2.0)),
        "residual": draw_residual(jax.random.fold_in(streams_of[17], 71), 0),
        "post_gain": jnp.clip(1.0 + 0.18 * jax.random.normal(streams_of[12], (D,), jnp.float32), 0.1, 1.9),
        "w_enc": normal_values(streams_of[13], (D, LATENTS), D ** -0.5, 0.125, ((0, 32), (1, 8))),
        "b_enc": normal_values(streams_of[14], (LATENTS,), 0.7, 4.0, ((0, 8),), jnp.float32),
        "w_dec": bell_draw_with(streams_of[15], (D, LATENTS), LATENTS ** -0.5, 0.09375, ((0, 32), (1, 8)), (1, 0, 32, 2.75)),
        "b_dec": normal_values(streams_of[16], (D,), 0.3, 2.0, ((0, 8),), jnp.float32),
    }


TOP_PRECISION = lax.Precision.HIGHEST
EPSILON = 1e-06

def convolve(padded, weights, tok_count):
    summed = weights[0] * padded[0:tok_count].astype(jnp.float32)
    for tap_index in range(1, weights.shape[0]):
        summed = summed + weights[tap_index] * padded[tap_index:tap_index + tok_count].astype(jnp.float32)
    return jax.nn.silu(summed)

def unit_heads(flat, head_count):
    shaped = flat.reshape(flat.shape[0], head_count, -1)
    return shaped * lax.rsqrt(lax.optimization_barrier(jnp.sum(shaped * shaped, axis=2, keepdims=True)) + EPSILON)

def to_blocks(tensor, length):
    tok_count, head_count, last_width = tensor.shape
    return tensor.reshape(tok_count // length, length, head_count, last_width).transpose(0, 2, 1, 3)

def head_blocks(tensor, length):
    head_count, tok_count = tensor.shape
    return tensor.reshape(head_count, tok_count // length, length).transpose(1, 0, 2)

def span_step(carry_state, inputs):
    queries, keys_in, values, beta_vals, decays = inputs
    length = queries.shape[1]
    cumulative = jnp.cumsum(decays, axis=1)
    spread = cumulative[:, :, None] - cumulative[:, None, :]
    row_ids = lax.broadcasted_iota(jnp.int32, (length, length), 0)
    col_ids = lax.broadcasted_iota(jnp.int32, (length, length), 1)
    within = jnp.where(col_ids <= row_ids, jnp.exp(jnp.minimum(spread, 0.0)), 0.0)
    before = jnp.where(col_ids < row_ids, within, 0.0)
    key_gram = jnp.einsum('hik,hjk->hij', keys_in, keys_in, precision=TOP_PRECISION)
    system = jnp.eye(length, dtype=jnp.float32) + beta_vals[:, :, None] * key_gram * before
    growth = jnp.exp(cumulative)
    targets = jnp.concatenate([beta_vals[:, :, None] * values, (beta_vals * growth)[:, :, None] * keys_in], axis=2)
    solved = lax.linalg.triangular_solve(system, targets, left_side=True, lower=True, unit_diagonal=True)
    val_width = values.shape[2]
    fresh_vals = solved[:, :, :val_width] - jnp.einsum('hik,hkw->hiw', solved[:, :, val_width:], carry_state, precision=TOP_PRECISION)
    scores = jnp.einsum('hik,hjk->hij', queries, keys_in, precision=TOP_PRECISION) * within
    output = growth[:, :, None] * jnp.einsum('hik,hkw->hiw', queries, carry_state, precision=TOP_PRECISION)
    output = output + jnp.einsum('hij,hjw->hiw', scores, fresh_vals, precision=TOP_PRECISION)
    remain = jnp.exp(cumulative[:, -1:] - cumulative)
    new_state = jnp.exp(cumulative[:, -1])[:, None, None] * carry_state
    new_state = new_state + jnp.einsum('hik,hiw->hkw', keys_in * remain[:, :, None], fresh_vals, precision=TOP_PRECISION)
    return (new_state, output)

def gate_norm(delta_out, z_gate, norm_gain):
    tok_count, head_count, val_width = delta_out.shape
    squares = lax.optimization_barrier(jnp.mean(delta_out * delta_out, axis=2, keepdims=True))
    gate_vals = jax.nn.silu(z_gate.reshape(tok_count, head_count, val_width).astype(jnp.float32))
    gated = delta_out * lax.rsqrt(squares + EPSILON) * norm_gain * gate_vals
    return gated.astype(jnp.bfloat16).reshape(tok_count, head_count * val_width)

def rms_norm(stream, post_gain):
    widened = stream.astype(jnp.float32)
    squares = lax.optimization_barrier(jnp.mean(widened * widened, axis=1, keepdims=True))
    return (widened * lax.rsqrt(squares + EPSILON) * post_gain).astype(jnp.bfloat16)

def reference(q_raw, k_raw, v_raw, z_gate, beta_raw, decay_log, conv_q, conv_k, conv_v, norm_gain, w_out, residual, post_gain, w_enc, b_enc, w_dec, b_dec):
    tok_count = q_raw.shape[0]
    joined = jnp.concatenate([q_raw, k_raw, v_raw], axis=1)
    padded = jnp.concatenate([jnp.zeros((CONV - 1, joined.shape[1]), jnp.bfloat16), joined], axis=0)
    weights = jnp.concatenate([conv_q, conv_k, conv_v], axis=1)
    mixed_conv = convolve(padded, weights, tok_count)
    key_width = HK * DK
    queries = unit_heads(mixed_conv[:, :key_width], HK) * DK ** (-0.5)
    keys_in = unit_heads(mixed_conv[:, key_width:2 * key_width], HK)
    values = mixed_conv[:, 2 * key_width:].reshape(tok_count, VALUE_HEADS, VALUE_HEAD_WIDTH)
    queries = jnp.repeat(queries, VALUE_HEADS // HK, axis=1)
    keys_in = jnp.repeat(keys_in, VALUE_HEADS // HK, axis=1)
    beta_vals = jax.nn.sigmoid(beta_raw)
    blocks = (to_blocks(queries, SPAN), to_blocks(keys_in, SPAN), to_blocks(values, SPAN), head_blocks(beta_vals, SPAN), head_blocks(decay_log, SPAN))
    start_state = jnp.zeros((VALUE_HEADS, DK, VALUE_HEAD_WIDTH), jnp.float32)
    final_state, output_list = lax.scan(span_step, start_state, blocks)
    delta_out = output_list.transpose(0, 2, 1, 3).reshape(tok_count, VALUE_HEADS, VALUE_HEAD_WIDTH)
    gated = gate_norm(delta_out, z_gate, norm_gain)
    attention = jnp.dot(gated.astype(jnp.float32), w_out.astype(jnp.float32), preferred_element_type=jnp.float32)
    stream = (residual.astype(jnp.float32) + attention).astype(jnp.bfloat16)
    normed = rms_norm(stream, post_gain)

    def transcode(pair):
        stream_rows, normed_rows = pair
        preact = jnp.dot(normed_rows.astype(jnp.float32), w_enc.astype(jnp.float32), preferred_element_type=jnp.float32) + b_enc
        latents = jax.nn.relu(preact).astype(jnp.bfloat16)
        decoded = lax.dot_general(latents.astype(jnp.float32), w_dec.astype(jnp.float32), (((1,), (1,)), ((), ())), preferred_element_type=jnp.float32)
        return (stream_rows.astype(jnp.float32) + decoded + b_dec).astype(jnp.bfloat16)
    block_count = tok_count // TOK_DEV
    result = lax.map(transcode, (stream.reshape(block_count, TOK_DEV, D), normed.reshape(block_count, TOK_DEV, D)))
    return result.reshape(tok_count, D)
```

```python
import functools

import jax
import jax.numpy as jnp
from jax import lax
from jax.experimental import pallas as pl
from jax.experimental.pallas import tpu as pltpu
from jax.sharding import PartitionSpec as P

F32 = jnp.float32
BF16 = jnp.bfloat16
EPSILON = 1e-06
T = 384
C = 128
H = 4
W = 128
ROW = 8
ROWS = 4
LAT = 8
TOP = lax.Precision.HIGHEST
MESH = pl.DeviceIdType.MESH
VMEM_LIMIT = 56 << 20


def mm(a, b, dims=((1,), (0,))):
    return lax.dot_general(
        a.astype(BF16), b.astype(BF16), (dims, ((), ())), preferred_element_type=F32
    )


def halves(a):
    high = a.astype(BF16)
    return high, (a - high.astype(F32)).astype(BF16)


def mm3(a, b, dims=((1,), (0,))):
    ah, al = a
    bh, bl = b
    dot = lambda x, y: lax.dot_general(x, y, (dims, ((), ())), preferred_element_type=F32)
    return dot(ah, bh) + (dot(ah, bl) + dot(al, bh))


def mm6(a, b, dims=((1,), (0,))):
    return lax.dot_general(a, b, (dims, ((), ())), precision=TOP, preferred_element_type=F32)


def silu(v):
    return v / (1.0 + jnp.exp(-v))


def triangular_inverses(systems, row, col):
    first = ((row & 1) == 1) & (col == row - 1)
    eye = (row == col).astype(F32)
    solved = [eye - jnp.where(first, a, 0.0) for a in systems]
    for level in range(1, 7):
        block_row, block_col = row >> level, col >> level
        mask = ((block_row & 1) == 1) & (block_col == block_row - 1)
        parts = [halves(x) for x in solved]
        below = [mm3(halves(jnp.where(mask, a, 0.0)), x) for a, x in zip(systems, parts)]
        solved = [x - mm3(p, halves(b)) for x, p, b in zip(solved, parts, below)]
    return solved


def remote(src, dst, send, recv, **where):
    return pltpu.make_async_remote_copy(
        src_ref=src,
        dst_ref=dst,
        send_sem=send,
        recv_sem=recv,
        device_id=where,
        device_id_type=MESH,
    )


def mixing_kernel(
    q_ref, k_ref, v_ref, z_ref, bd_ref, wc_ref, gain_ref, wout_ref,
    part_ref,
    halo, pad, qs, ks, vs, ql, ol, comp, acur, msg, slots, prefix, aprefix, tot, tslots, sout, sin,
    hs, hr, ms, mr, ts, tr, ss, sr,
):
    seq = lax.axis_index("seq")
    n_seq = ROW * ROWS
    right, left = lax.rem(seq + 1, n_seq), lax.rem(seq + n_seq - 1, n_seq)
    y, j = seq // ROW, lax.rem(seq, ROW)
    zh, core = j // 2, lax.rem(j, 2)
    base = y * ROW

    barrier = pltpu.get_barrier_semaphore()
    pl.semaphore_signal(barrier, inc=1, device_id={"seq": right}, device_id_type=MESH)
    pl.semaphore_signal(barrier, inc=1, device_id={"seq": left}, device_id_type=MESH)
    for d in range(1, ROW):
        peer = base + lax.rem(j + d, ROW)
        pl.semaphore_signal(barrier, inc=1, device_id={"seq": peer}, device_id_type=MESH)
    for d in range(1, ROWS):
        peer = lax.rem(y + d, ROWS) * ROW + j
        pl.semaphore_signal(barrier, inc=1, device_id={"seq": peer}, device_id_type=MESH)
    pl.semaphore_wait(barrier, 2 + ROW - 1 + ROWS - 1)

    halos = []
    for i, (ref, lo, width) in enumerate(((q_ref, 0, 256), (k_ref, 256, 256), (v_ref, 512, 512))):
        halos.append(
            remote(
                ref.at[pl.ds(T - 16, 16), :],
                halo.at[:, pl.ds(lo, width)],
                hs.at[i], hr.at[i], seq=right,
            )
        )
        halos[-1].start()
        pad[pl.ds(16, T), lo : lo + width] = ref[...].astype(F32)
    for copy in halos:
        copy.wait()
    pad[pl.ds(0, 16), :] = jnp.where(seq == 0, 0.0, halo[...].astype(F32))

    for g in range(8):
        cols = slice(g * W, (g + 1) * W)
        total = wc_ref[0:1, cols] * pad[13 : 13 + T, cols]
        for tap in range(1, 4):
            total = total + wc_ref[tap : tap + 1, cols] * pad[13 + tap : 13 + tap + T, cols]
        total = silu(total)
        if g < 4:
            total = total * lax.rsqrt(jnp.sum(total * total, axis=1, keepdims=True) + EPSILON)
        if g < 2:
            qs[:, cols] = total * (W**-0.5)
        elif g < 4:
            ks[:, (g - 2) * W : (g - 1) * W] = total
        else:
            vs[:, (g - 4) * W : (g - 3) * W] = total

    row = lax.broadcasted_iota(jnp.int32, (C, C), 0)
    col = lax.broadcasted_iota(jnp.int32, (C, C), 1)
    lower = (col <= row).astype(F32)
    upper = (row <= col).astype(F32)
    eye = (row == col).astype(F32)
    ones = jnp.ones((C, C), F32)
    comp[...] = jnp.zeros_like(comp)
    acur[...] = jnp.ones_like(acur)

    def block(c, _):
        rows = pl.ds(pl.multiple_of(c * C, C), C)
        bd = bd_ref[c]
        beta_col = mm6(eye, 1.0 / (1.0 + jnp.exp(-bd)), ((1,), (1,)))
        cum_col = mm6(lower, bd, ((1,), (1,)))
        cum_row = mm6(bd, upper)
        tot_row = mm6(bd, ones)
        systems, scores, keys, queries = [], [], [], []
        for kh in range(2):
            k = ks[rows, kh * W : (kh + 1) * W]
            q = qs[rows, kh * W : (kh + 1) * W]
            kp, qp = halves(k), halves(q)
            gram = mm3(kp, kp, ((1,), (1,)))
            score = mm3(qp, kp, ((1,), (1,)))
            keys.append(k)
            queries.append(q)
            for h in (2 * kh, 2 * kh + 1):
                spread = cum_col[:, 4 + h : 5 + h] - cum_row[4 + h : 5 + h, :]
                within = jnp.where(col <= row, jnp.exp(jnp.minimum(spread, 0.0)), 0.0)
                systems.append(
                    jnp.where(col < row, beta_col[:, h : h + 1] * gram * within, 0.0)
                )
                scores.append(score * within)
        solved = triangular_inverses(systems, row, col)
        key_t = [k.T for k in keys]
        for h in range(H):
            kh = h // 2
            beta = beta_col[:, h : h + 1]
            growth = jnp.exp(cum_col[:, 4 + h : 5 + h])
            v = vs[rows, h * W : (h + 1) * W]
            targets = jnp.concatenate([beta * v, (beta * growth) * keys[kh]], axis=1)
            fresh = mm(solved[h], targets).astype(BF16)
            out = mm(scores[h], fresh)
            q_map = growth * queries[kh] - out[:, W:]
            total = tot_row[4 + h : 5 + h, :]
            decay = jnp.exp(total)
            remain = jnp.exp(total - cum_row[4 + h : 5 + h, :])
            new = mm(key_t[kh] * remain, fresh)
            so_far = comp[h]
            a = acur[h, 0:1, :]
            read = mm(q_map, so_far)
            ql[h, rows, :] = (a * q_map - read[:, W:]).astype(BF16)
            ol[h, rows, :] = out[:, :W] + read[:, :W]
            turned = mm(new[:, W:], so_far)
            decay2 = jnp.concatenate([decay, decay], axis=1)
            comp[h] = (
                decay2 * so_far - turned + jnp.concatenate([new[:, :W], a * new[:, W:]], axis=1)
            )
            acur[h] = jnp.broadcast_to(a * decay, (8, W))
        return 0

    lax.fori_loop(0, T // C, block, 0)

    def split_row(a):
        high = a.astype(BF16).astype(F32)
        mid = (a - high).astype(BF16).astype(F32)
        low = a - high - mid
        r = lax.broadcasted_iota(jnp.int32, (16, W), 0)
        block = jnp.where(r == 0, high, jnp.where(r == 1, mid, jnp.where(r == 2, low, 0.0)))
        return jnp.concatenate([block, block], axis=1).astype(BF16)

    def joined_row(ref):
        return jnp.sum(ref[C : C + 16, :W].astype(F32), axis=0, keepdims=True)

    for h in range(H):
        msg[h, :C, :] = comp[h].astype(BF16)
        msg[h, C:, :] = split_row(acur[h, 0:1, :])

    def to_handler(h):
        return remote(msg.at[h], slots.at[j], ms.at[h], mr.at[j], seq=base + 2 * h)

    for h in range(H):

        @pl.when(j != 2 * h)
        def _():
            to_handler(h).start()

        @pl.when(j == 2 * h)
        def _():
            slots[j] = msg[h]

    def total_to(d):
        peer = lax.rem(y + d, ROWS)
        return remote(tot, tslots.at[y], ts.at[d - 1], tr.at[y], seq=peer * ROW + j)

    def state_to(i):
        return remote(sout.at[i], sin.at[zh], ss.at[i], sr.at[zh], seq=base + i)

    @pl.when(core == 0)
    def _():
        for i in range(ROW):

            @pl.when(i != j)
            def _():
                remote(msg.at[0], slots.at[i], ms.at[0], mr.at[i], seq=base + i).wait_recv()

            maps = slots[i, :C, :]
            a_new = joined_row(slots.at[i])
            if i == 0:
                now, a_now = maps.astype(F32), a_new
            else:
                a_old, old = aprefix[i - 1, 0:1, :], prefix[i - 1]
                turned = mm(maps[:, W:], old)
                new = maps.astype(F32)
                a2 = jnp.concatenate([a_new, a_new], axis=1)
                now = (
                    a2 * old - turned + jnp.concatenate([new[:, :W], a_old * new[:, W:]], axis=1)
                )
                a_now = a_old * a_new
            prefix[i] = now
            aprefix[i] = jnp.broadcast_to(a_now, (8, W))
        tot[:C, :] = prefix[ROW - 1].astype(BF16)
        tot[C:, :] = split_row(aprefix[ROW - 1, 0:1, :])
        for d in range(1, ROWS):
            total_to(d).start()
        tslots[y] = tot[...]
        state = jnp.zeros((C, W), F32)
        for i in range(ROWS):

            @pl.when(i != y)
            def _():
                remote(tot, tslots.at[i], ts.at[0], tr.at[i], seq=i * ROW + j).wait_recv()

            maps = tslots[i]
            later = (
                joined_row(tslots.at[i]) * state
                - mm(maps[:C, W:], state)
                + maps[:C, :W].astype(F32)
            )
            state = jnp.where(i < y, later, state)
        for i in range(ROW):
            if i == 0:
                mine = state
            else:
                mine = (
                    aprefix[i - 1, 0:1, :] * state
                    - mm(prefix[i - 1, :, W:], state)
                    + prefix[i - 1, :, :W]
                )
            sout[i] = mine.astype(BF16)

            @pl.when(i != j)
            def _():
                state_to(i).start()

            @pl.when(i == j)
            def _():
                sin[zh] = sout[i]

    gated = []
    for h in range(H):

        @pl.when(j != 2 * h)
        def _():
            remote(sout.at[0], sin.at[h], ss.at[0], sr.at[h], seq=base + 2 * h).wait_recv()

        delta = ol[h] + mm(ql[h], sin[h])
        squares = jnp.mean(delta * delta, axis=1, keepdims=True)
        gate = silu(z_ref[:, h * W : (h + 1) * W].astype(F32))
        gated.append((delta * lax.rsqrt(squares + EPSILON) * gain_ref[...] * gate).astype(BF16))
    gated = jnp.concatenate(gated, axis=1)
    for lane in range(LAT):
        part_ref[lane] = mm(gated, wout_ref[:, lane * 256 : (lane + 1) * 256]).astype(BF16)

    for h in range(H):

        @pl.when(j != 2 * h)
        def _():
            to_handler(h).wait_send()

    @pl.when(core == 0)
    def _():
        for d in range(1, ROWS):
            total_to(d).wait_send()
        for i in range(ROW):

            @pl.when(i != j)
            def _():
                state_to(i).wait_send()


def mixing(q, k, v, z, bd, wc, gain, wout):
    return pl.pallas_call(
        mixing_kernel,
        out_shape=jax.ShapeDtypeStruct((LAT, T, 256), BF16),
        in_specs=[pl.BlockSpec(memory_space=pltpu.VMEM)] * 8,
        out_specs=pl.BlockSpec(memory_space=pltpu.VMEM),
        scratch_shapes=[
            pltpu.VMEM((16, 1024), BF16),
            pltpu.VMEM((T + 16, 1024), F32),
            pltpu.VMEM((T, 256), F32),
            pltpu.VMEM((T, 256), F32),
            pltpu.VMEM((T, 512), F32),
            pltpu.VMEM((H, T, W), BF16),
            pltpu.VMEM((H, T, W), F32),
            pltpu.VMEM((H, C, 2 * W), F32),
            pltpu.VMEM((H, 8, W), F32),
            pltpu.VMEM((H, C + 16, 2 * W), BF16),
            pltpu.VMEM((ROW, C + 16, 2 * W), BF16),
            pltpu.VMEM((ROW, C, 2 * W), F32),
            pltpu.VMEM((ROW, 8, W), F32),
            pltpu.VMEM((C + 16, 2 * W), BF16),
            pltpu.VMEM((ROWS, C + 16, 2 * W), BF16),
            pltpu.VMEM((ROW, C, W), BF16),
            pltpu.VMEM((H, C, W), BF16),
            pltpu.SemaphoreType.DMA((3,)),
            pltpu.SemaphoreType.DMA((3,)),
            pltpu.SemaphoreType.DMA((H,)),
            pltpu.SemaphoreType.DMA((ROW,)),
            pltpu.SemaphoreType.DMA((ROWS - 1,)),
            pltpu.SemaphoreType.DMA((ROWS,)),
            pltpu.SemaphoreType.DMA((ROW,)),
            pltpu.SemaphoreType.DMA((H,)),
        ],
        compiler_params=pltpu.CompilerParams(
            collective_id=0, has_side_effects=True, vmem_limit_bytes=VMEM_LIMIT
        ),
        cost_estimate=pl.CostEstimate(
            flops=100_000_000_000, bytes_accessed=8_000_000, transcendentals=0
        ),
        name="mixing",
    )(q, k, v, z, bd, wc, gain, wout)


def transcoder_kernel(
    part_ref, res_ref, gain_ref, benc_ref, bdec_ref, wenc_hbm, wdec_hbm,
    out_ref,
    wenc, wdec, arrived, streams, normed, latents, decoded, returned,
    wsem, s1, r1, s2, r2, s3, r3,
):
    me = lax.axis_index("lat")
    load_enc = pltpu.make_async_copy(wenc_hbm, wenc, wsem.at[0])
    load_dec = pltpu.make_async_copy(wdec_hbm, wdec, wsem.at[1])
    load_enc.start()
    load_dec.start()

    barrier = pltpu.get_barrier_semaphore()
    for d in range(1, LAT):
        peer = lax.rem(me + d, LAT)
        pl.semaphore_signal(barrier, inc=1, device_id={"lat": peer}, device_id_type=MESH)
    pl.semaphore_wait(barrier, LAT - 1)

    def peer_at(d):
        return lax.rem(me + d, LAT)

    def scatter(d):
        return remote(part_ref.at[peer_at(d)], arrived.at[me], s1.at[d - 1], r1.at[me], lat=peer_at(d))

    def gather(d):
        return remote(streams.at[me], streams.at[me], s2.at[d - 1], r2.at[me], lat=peer_at(d))

    def scatter_back(d):
        return remote(decoded.at[peer_at(d)], returned.at[me], s3.at[d - 1], r3.at[me], lat=peer_at(d))

    for d in range(1, LAT):
        scatter(d).start()
    attention = part_ref[me].astype(F32)
    for d in range(1, LAT):
        p = peer_at(d)
        remote(part_ref.at[p], arrived.at[p], s1.at[0], r1.at[p], lat=p).wait_recv()
        attention = attention + arrived[p].astype(F32)
    streams[me] = (res_ref[...].astype(F32) + attention).astype(BF16)
    for d in range(1, LAT):
        gather(d).start()
    own = streams[me].astype(F32)
    squares = jnp.sum(own * own, axis=1, keepdims=True)
    for d in range(1, LAT):
        p = peer_at(d)
        remote(streams.at[p], streams.at[p], s2.at[0], r2.at[p], lat=p).wait_recv()
        wide = streams[p].astype(F32)
        squares = squares + jnp.sum(wide * wide, axis=1, keepdims=True)
    scale = lax.rsqrt(squares * (1.0 / 2048.0) + EPSILON)
    for l in range(LAT):
        cols = slice(l * 256, (l + 1) * 256)
        normed[:, cols] = (streams[l].astype(F32) * scale * gain_ref[:, cols]).astype(BF16)
    load_enc.wait()

    def encode(i, _):
        cols = pl.ds(pl.multiple_of(i * 256, 256), 256)
        pre = jnp.dot(normed[...], wenc[:, cols], preferred_element_type=F32) + benc_ref[:, cols]
        latents[:, cols] = jnp.maximum(pre, 0.0).astype(BF16)
        return 0

    lax.fori_loop(0, LAT, encode, 0)
    load_dec.wait()

    def decode(p):
        rows = pl.ds(pl.multiple_of(p * 256, 256), 256)
        return lax.dot_general(
            latents[...], wdec[rows, :], (((1,), (1,)), ((), ())), preferred_element_type=F32
        )

    def decode_step(d, _):
        p = peer_at(d)
        decoded[p] = decode(p).astype(BF16)
        scatter_back(d).start()
        return 0

    lax.fori_loop(1, LAT, decode_step, 0)
    total = decode(me) + streams[me].astype(F32) + bdec_ref[...]
    for d in range(1, LAT):
        p = peer_at(d)
        remote(decoded.at[p], returned.at[p], s3.at[0], r3.at[p], lat=p).wait_recv()
        total = total + returned[p].astype(F32)
    out_ref[...] = total.astype(BF16)
    for d in range(1, LAT):
        scatter(d).wait_send()
        gather(d).wait_send()
        scatter_back(d).wait_send()


def transcoder(part, residual, gain, benc, bdec, wenc, wdec):
    vmem = pl.BlockSpec(memory_space=pltpu.VMEM)
    block = pltpu.VMEM((LAT, T, 256), BF16)
    return pl.pallas_call(
        transcoder_kernel,
        out_shape=jax.ShapeDtypeStruct((T, 256), BF16),
        in_specs=[vmem] * 5 + [pl.BlockSpec(memory_space=pl.ANY)] * 2,
        out_specs=vmem,
        scratch_shapes=[
            pltpu.VMEM((2048, 2048), BF16),
            pltpu.VMEM((2048, 2048), BF16),
            block,
            block,
            pltpu.VMEM((T, 2048), BF16),
            pltpu.VMEM((T, 2048), BF16),
            block,
            block,
            pltpu.SemaphoreType.DMA((2,)),
        ]
        + [pltpu.SemaphoreType.DMA((LAT - 1,)), pltpu.SemaphoreType.DMA((LAT,))] * 3,
        compiler_params=pltpu.CompilerParams(
            collective_id=1, has_side_effects=True, vmem_limit_bytes=VMEM_LIMIT
        ),
        cost_estimate=pl.CostEstimate(
            flops=6_442_450_944, bytes_accessed=20_000_000, transcendentals=0
        ),
        name="transcoder",
    )(part, residual, gain, benc, bdec, wenc, wdec)


def per_device(
    q_raw,
    k_raw,
    v_raw,
    z_gate,
    beta_raw,
    decay_log,
    conv_q,
    conv_k,
    conv_v,
    norm_gain,
    w_out,
    residual,
    post_gain,
    w_enc,
    b_enc,
    w_dec,
    b_dec,
):
    bd = jnp.concatenate([beta_raw, decay_log], axis=0)
    bd = bd.reshape(8, T // C, C).transpose(1, 0, 2)
    wc = jnp.concatenate([conv_q, conv_k, conv_v], axis=1)
    wenc = lax.all_gather(w_enc, "seq", axis=0, tiled=True)
    wdec = lax.all_gather(w_dec, "seq", axis=0, tiled=True)
    part = mixing(q_raw, k_raw, v_raw, z_gate, bd, wc, norm_gain[None, :], w_out)
    return transcoder(
        part, residual, post_gain[None, :], b_enc[None, :], b_dec[None, :], wenc, wdec
    )


def solution(mesh):
    return jax.shard_map(
        per_device,
        mesh=mesh,
        in_specs=(
            P("seq", "lat"),
            P("seq", "lat"),
            P("seq", "lat"),
            P("seq", "lat"),
            P("lat", "seq"),
            P("lat", "seq"),
            P(None, "lat"),
            P(None, "lat"),
            P(None, "lat"),
            P(),
            P("lat", None),
            P("seq", "lat"),
            P(),
            P("seq", "lat"),
            P("lat"),
            P("seq", "lat"),
            P("lat"),
        ),
        out_specs=P("seq", "lat"),
        check_vma=False,
    )
```

```python
import functools

import jax
import jax.numpy as jnp
from jax import lax
from jax.experimental import pallas as pl
from jax.experimental.pallas import tpu as pltpu
from jax.sharding import PartitionSpec as P

F32 = jnp.float32
BF16 = jnp.bfloat16
EPSILON = 1e-06
T = 384
C = 128
H = 4
W = 128
ROW = 8
ROWS = 4
LAT = 8
TOP = lax.Precision.HIGHEST
MESH = pl.DeviceIdType.MESH
VMEM_LIMIT = 56 << 20


def mm(a, b, dims=((1,), (0,))):
    return lax.dot_general(
        a.astype(BF16), b.astype(BF16), (dims, ((), ())), preferred_element_type=F32
    )


def halves(a):
    high = a.astype(BF16)
    return high, (a - high.astype(F32)).astype(BF16)


def mm3(a, b, dims=((1,), (0,))):
    ah, al = a
    bh, bl = b
    dot = lambda x, y: lax.dot_general(x, y, (dims, ((), ())), preferred_element_type=F32)
    return dot(ah, bh) + (dot(ah, bl) + dot(al, bh))


def mm6(a, b, dims=((1,), (0,))):
    return lax.dot_general(a, b, (dims, ((), ())), precision=TOP, preferred_element_type=F32)


def silu(v):
    return v / (1.0 + jnp.exp(-v))


def triangular_inverses(systems, row, col):
    first = ((row & 1) == 1) & (col == row - 1)
    eye = (row == col).astype(F32)
    solved = [eye - jnp.where(first, a, 0.0) for a in systems]
    for level in range(1, 7):
        block_row, block_col = row >> level, col >> level
        mask = ((block_row & 1) == 1) & (block_col == block_row - 1)
        parts = [halves(x) for x in solved]
        below = [mm3(halves(jnp.where(mask, a, 0.0)), x) for a, x in zip(systems, parts)]
        solved = [x - mm3(p, halves(b)) for x, p, b in zip(solved, parts, below)]
    return solved


def remote(src, dst, send, recv, **where):
    return pltpu.make_async_remote_copy(
        src_ref=src,
        dst_ref=dst,
        send_sem=send,
        recv_sem=recv,
        device_id=where,
        device_id_type=MESH,
    )


def layer_kernel(
    q_ref, k_ref, v_ref, z_ref, bd_ref, wc_ref, gain_ref,
    res_ref, pgain_ref, benc_ref, bdec_ref, wout_hbm, wenc_hbm, wdec_hbm,
    out_ref,
    halo, pad, qs, ks, vs, ql, ol, comp, acur, msg, slots, prefix, aprefix, tot, tslots, sout, sin,
    wout_ref, wenc, wdec, part_ref, arrived, streams, normed, latents, decoded, returned,
    hs, hr, ms, mr, ts, tr, ss, sr,
    wsem, s1, r1, s2, r2, s3, r3,
    gr, cr, cs, z1s, z2s, y1s, y2s,
):
    seq = lax.axis_index("seq")
    me = lax.axis_index("lat")
    n_seq = ROW * ROWS
    right, left = lax.rem(seq + 1, n_seq), lax.rem(seq + n_seq - 1, n_seq)
    y, j = seq // ROW, lax.rem(seq, ROW)
    zh, core = j // 2, lax.rem(j, 2)
    base = y * ROW

    barrier = pltpu.get_barrier_semaphore()
    pl.semaphore_signal(barrier, inc=1, device_id={"seq": right}, device_id_type=MESH)
    pl.semaphore_signal(barrier, inc=1, device_id={"seq": left}, device_id_type=MESH)
    for d in range(1, ROW):
        peer = base + lax.rem(j + d, ROW)
        pl.semaphore_signal(barrier, inc=1, device_id={"seq": peer}, device_id_type=MESH)
    for d in range(1, ROWS):
        peer = lax.rem(y + d, ROWS) * ROW + j
        pl.semaphore_signal(barrier, inc=1, device_id={"seq": peer}, device_id_type=MESH)
    for d in range(1, LAT):
        peer = lax.rem(me + d, LAT)
        pl.semaphore_signal(barrier, inc=1, device_id={"lat": peer}, device_id_type=MESH)
    pl.semaphore_wait(barrier, 2 + ROW - 1 + ROWS - 1 + LAT - 1)

    full, own_shard = (wenc, wdec), (wenc_hbm, wdec_hbm)
    sibling = base + 2 * zh + 1 - core

    def shard_id(dy, dz):
        return lax.rem(y + dy, ROWS) * 4 + lax.rem(zh + dz, 4)

    def shard(a, s, c):
        return full[a].at[pl.ds(pl.multiple_of((s * 2 + c) * 64, 64), 64), :]

    def seq_at(dy, dz):
        return shard_id(dy, dz) * 2 + core

    def passed(a, s, sem, to):
        return remote(shard(a, s, core), shard(a, s, core), sem, gr.at[a, s], seq=to)

    def along_z(a, up):
        to = seq_at(0, 1 if up else 3)
        here = shard(a, shard_id(0, 0), core)
        return remote(own_shard[a], here, z1s.at[a, int(up)], gr.at[a, shard_id(0, 0)], seq=to)

    def along_z_on(a):
        return passed(a, shard_id(0, 3 if a == 0 else 1), z2s.at[a], seq_at(0, 1 if a == 0 else 3))

    def along_y(a, dz, up):
        s, to, sem = shard_id(0, dz), seq_at(1 if up else 3, 0), y1s.at[a, dz, int(up)]
        if dz == 0:
            return remote(own_shard[a], shard(a, s, core), sem, gr.at[a, s], seq=to)
        return passed(a, s, sem, to)

    def along_y_on(a, dz):
        s = shard_id(3 if a == 0 else 1, dz)
        return passed(a, s, y2s.at[a, dz], seq_at(1 if a == 0 else 3, 0))

    def across(a, dy, dz):
        s = shard_id(dy, dz)
        src = own_shard[a] if dy == 0 and dz == 0 else shard(a, s, core)
        return remote(src, shard(a, s, core), cs.at[a, s], cr.at[a, s], seq=sibling)

    def landed(a, dy, dz):
        s = shard_id(dy, dz)
        remote(shard(a, s, core), shard(a, s, core), cs.at[a, s], gr.at[a, s], seq=sibling).wait_recv()

    def landed_across(a, dy, dz):
        s = shard_id(dy, dz)
        there = shard(a, s, 1 - core)
        remote(there, there, cs.at[a, s], cr.at[a, s], seq=sibling).wait_recv()

    def from_z(a, dz):
        landed(a, 0, dz)
        along_y(a, dz, True).start()
        along_y(a, dz, False).start()
        across(a, 0, dz).start()

    def from_y(a, dz):
        for dy in (3, 1) if a == 0 else (1, 3):
            landed(a, dy, dz)
            if dy == (3 if a == 0 else 1):
                along_y_on(a, dz).start()
            across(a, dy, dz).start()

    def from_y_on(a, dz):
        landed(a, 2, dz)
        across(a, 2, dz).start()

    loads = [
        pltpu.make_async_copy(wenc_hbm, shard(0, shard_id(0, 0), core), wsem.at[0]),
        pltpu.make_async_copy(wdec_hbm, shard(1, shard_id(0, 0), core), wsem.at[1]),
        pltpu.make_async_copy(wout_hbm, wout_ref, wsem.at[2]),
    ]
    halos = []
    for i, (ref, lo, width) in enumerate(((q_ref, 0, 256), (k_ref, 256, 256), (v_ref, 512, 512))):
        halos.append(
            remote(
                ref.at[pl.ds(T - 16, 16), :],
                halo.at[:, pl.ds(lo, width)],
                hs.at[i], hr.at[i], seq=right,
            )
        )
        halos[-1].start()
        pad[pl.ds(16, T), lo : lo + width] = ref[...].astype(F32)
    for a in range(2):
        for up in (True, False):
            along_z(a, up).start()
            along_y(a, 0, up).start()
        across(a, 0, 0).start()
    for copy in loads:
        copy.start()
    for copy in halos:
        copy.wait()
    pad[pl.ds(0, 16), :] = jnp.where(seq == 0, 0.0, halo[...].astype(F32))

    for g in range(8):
        cols = slice(g * W, (g + 1) * W)
        total = wc_ref[0:1, cols] * pad[13 : 13 + T, cols]
        for tap in range(1, 4):
            total = total + wc_ref[tap : tap + 1, cols] * pad[13 + tap : 13 + tap + T, cols]
        total = silu(total)
        if g < 4:
            total = total * lax.rsqrt(jnp.sum(total * total, axis=1, keepdims=True) + EPSILON)
        if g < 2:
            qs[:, cols] = total * (W**-0.5)
        elif g < 4:
            ks[:, (g - 2) * W : (g - 1) * W] = total
        else:
            vs[:, (g - 4) * W : (g - 3) * W] = total

    from_z(0, 3)
    along_z_on(0).start()
    from_z(0, 1)

    row = lax.broadcasted_iota(jnp.int32, (C, C), 0)
    col = lax.broadcasted_iota(jnp.int32, (C, C), 1)
    lower = (col <= row).astype(F32)
    upper = (row <= col).astype(F32)
    eye = (row == col).astype(F32)
    ones = jnp.ones((C, C), F32)
    comp[...] = jnp.zeros_like(comp)
    acur[...] = jnp.ones_like(acur)

    def block(c, _):
        rows = pl.ds(pl.multiple_of(c * C, C), C)
        bd = bd_ref[c]
        beta_col = mm6(eye, 1.0 / (1.0 + jnp.exp(-bd)), ((1,), (1,)))
        cum_col = mm6(lower, bd, ((1,), (1,)))
        cum_row = mm6(bd, upper)
        tot_row = mm6(bd, ones)
        systems, scores, keys, queries = [], [], [], []
        for kh in range(2):
            k = ks[rows, kh * W : (kh + 1) * W]
            q = qs[rows, kh * W : (kh + 1) * W]
            kp, qp = halves(k), halves(q)
            gram = mm3(kp, kp, ((1,), (1,)))
            score = mm3(qp, kp, ((1,), (1,)))
            keys.append(k)
            queries.append(q)
            for h in (2 * kh, 2 * kh + 1):
                spread = cum_col[:, 4 + h : 5 + h] - cum_row[4 + h : 5 + h, :]
                within = jnp.where(col <= row, jnp.exp(jnp.minimum(spread, 0.0)), 0.0)
                systems.append(
                    jnp.where(col < row, beta_col[:, h : h + 1] * gram * within, 0.0)
                )
                scores.append(score * within)
        solved = triangular_inverses(systems, row, col)
        key_t = [k.T for k in keys]
        for h in range(H):
            kh = h // 2
            beta = beta_col[:, h : h + 1]
            growth = jnp.exp(cum_col[:, 4 + h : 5 + h])
            v = vs[rows, h * W : (h + 1) * W]
            targets = jnp.concatenate([beta * v, (beta * growth) * keys[kh]], axis=1)
            fresh = mm(solved[h], targets).astype(BF16)
            out = mm(scores[h], fresh)
            q_map = growth * queries[kh] - out[:, W:]
            total = tot_row[4 + h : 5 + h, :]
            decay = jnp.exp(total)
            remain = jnp.exp(total - cum_row[4 + h : 5 + h, :])
            new = mm(key_t[kh] * remain, fresh)
            so_far = comp[h]
            a = acur[h, 0:1, :]
            read = mm(q_map, so_far)
            ql[h, rows, :] = (a * q_map - read[:, W:]).astype(BF16)
            ol[h, rows, :] = out[:, :W] + read[:, :W]
            turned = mm(new[:, W:], so_far)
            decay2 = jnp.concatenate([decay, decay], axis=1)
            comp[h] = (
                decay2 * so_far - turned + jnp.concatenate([new[:, :W], a * new[:, W:]], axis=1)
            )
            acur[h] = jnp.broadcast_to(a * decay, (8, W))

        @pl.when(c == 0)
        def _():
            from_z(1, 1)
            along_z_on(1).start()
            from_z(1, 3)
            from_y(0, 0)
            from_y(1, 0)

        @pl.when(c == 1)
        def _():
            from_z(0, 2)
            from_z(1, 2)

        return 0

    lax.fori_loop(0, T // C, block, 0)

    def split_row(a):
        high = a.astype(BF16).astype(F32)
        mid = (a - high).astype(BF16).astype(F32)
        low = a - high - mid
        r = lax.broadcasted_iota(jnp.int32, (16, W), 0)
        block = jnp.where(r == 0, high, jnp.where(r == 1, mid, jnp.where(r == 2, low, 0.0)))
        return jnp.concatenate([block, block], axis=1).astype(BF16)

    def joined_row(ref):
        return jnp.sum(ref[C : C + 16, :W].astype(F32), axis=0, keepdims=True)

    for h in range(H):
        msg[h, :C, :] = comp[h].astype(BF16)
        msg[h, C:, :] = split_row(acur[h, 0:1, :])

    def to_handler(h):
        return remote(msg.at[h], slots.at[j], ms.at[h], mr.at[j], seq=base + 2 * h)

    for h in range(H):

        @pl.when(j != 2 * h)
        def _():
            to_handler(h).start()

        @pl.when(j == 2 * h)
        def _():
            slots[j] = msg[h]

    from_y(0, 1)
    from_y(0, 3)

    def total_to(d):
        peer = lax.rem(y + d, ROWS)
        return remote(tot, tslots.at[y], ts.at[d - 1], tr.at[y], seq=peer * ROW + j)

    def state_to(i):
        return remote(sout.at[i], sin.at[zh], ss.at[i], sr.at[zh], seq=base + i)

    @pl.when(core == 0)
    def _():
        for i in range(ROW):

            @pl.when(i != j)
            def _():
                remote(msg.at[0], slots.at[i], ms.at[0], mr.at[i], seq=base + i).wait_recv()

            maps = slots[i, :C, :]
            a_new = joined_row(slots.at[i])
            if i == 0:
                now, a_now = maps.astype(F32), a_new
            else:
                a_old, old = aprefix[i - 1, 0:1, :], prefix[i - 1]
                turned = mm(maps[:, W:], old)
                new = maps.astype(F32)
                a2 = jnp.concatenate([a_new, a_new], axis=1)
                now = (
                    a2 * old - turned + jnp.concatenate([new[:, :W], a_old * new[:, W:]], axis=1)
                )
                a_now = a_old * a_new
            prefix[i] = now
            aprefix[i] = jnp.broadcast_to(a_now, (8, W))
        tot[:C, :] = prefix[ROW - 1].astype(BF16)
        tot[C:, :] = split_row(aprefix[ROW - 1, 0:1, :])
        for d in range(1, ROWS):
            total_to(d).start()
        tslots[y] = tot[...]
        state = jnp.zeros((C, W), F32)
        for i in range(ROWS):

            @pl.when(i != y)
            def _():
                remote(tot, tslots.at[i], ts.at[0], tr.at[i], seq=i * ROW + j).wait_recv()

            maps = tslots[i]
            later = (
                joined_row(tslots.at[i]) * state
                - mm(maps[:C, W:], state)
                + maps[:C, :W].astype(F32)
            )
            state = jnp.where(i < y, later, state)
        for i in range(ROW):
            if i == 0:
                mine = state
            else:
                mine = (
                    aprefix[i - 1, 0:1, :] * state
                    - mm(prefix[i - 1, :, W:], state)
                    + prefix[i - 1, :, :W]
                )
            sout[i] = mine.astype(BF16)

            @pl.when(i != j)
            def _():
                state_to(i).start()

            @pl.when(i == j)
            def _():
                sin[zh] = sout[i]

    from_y(1, 1)
    from_y(1, 3)

    gated = []
    for h in range(H):

        @pl.when(j != 2 * h)
        def _():
            remote(sout.at[0], sin.at[h], ss.at[0], sr.at[h], seq=base + 2 * h).wait_recv()

        delta = ol[h] + mm(ql[h], sin[h])
        squares = jnp.mean(delta * delta, axis=1, keepdims=True)
        gate = silu(z_ref[:, h * W : (h + 1) * W].astype(F32))
        gated.append((delta * lax.rsqrt(squares + EPSILON) * gain_ref[...] * gate).astype(BF16))
    gated = jnp.concatenate(gated, axis=1)
    for copy in loads:
        copy.wait()
    for lane in range(LAT):
        part_ref[lane] = mm(gated, wout_ref[:, lane * 256 : (lane + 1) * 256]).astype(BF16)

    for h in range(H):

        @pl.when(j != 2 * h)
        def _():
            to_handler(h).wait_send()

    @pl.when(core == 0)
    def _():
        for d in range(1, ROWS):
            total_to(d).wait_send()
        for i in range(ROW):

            @pl.when(i != j)
            def _():
                state_to(i).wait_send()

    def peer_at(d):
        return lax.rem(me + d, LAT)

    def scatter(d):
        return remote(part_ref.at[peer_at(d)], arrived.at[me], s1.at[d - 1], r1.at[me], lat=peer_at(d))

    def gather(d):
        return remote(streams.at[me], streams.at[me], s2.at[d - 1], r2.at[me], lat=peer_at(d))

    def scatter_back(d):
        return remote(decoded.at[peer_at(d)], returned.at[me], s3.at[d - 1], r3.at[me], lat=peer_at(d))

    for d in range(1, LAT):
        scatter(d).start()
    from_y(0, 2)
    from_y(1, 2)
    attention = part_ref[me].astype(F32)
    for d in range(1, LAT):
        p = peer_at(d)
        remote(part_ref.at[p], arrived.at[p], s1.at[0], r1.at[p], lat=p).wait_recv()
        attention = attention + arrived[p].astype(F32)
    streams[me] = (res_ref[...].astype(F32) + attention).astype(BF16)
    for d in range(1, LAT):
        gather(d).start()
    for dz in range(4):
        for a in range(2):
            from_y_on(a, dz)
    own = streams[me].astype(F32)
    squares = jnp.sum(own * own, axis=1, keepdims=True)
    for d in range(1, LAT):
        p = peer_at(d)
        remote(streams.at[p], streams.at[p], s2.at[0], r2.at[p], lat=p).wait_recv()
        wide = streams[p].astype(F32)
        squares = squares + jnp.sum(wide * wide, axis=1, keepdims=True)
    scale = lax.rsqrt(squares * (1.0 / 2048.0) + EPSILON)
    for l in range(LAT):
        cols = slice(l * 256, (l + 1) * 256)
        normed[:, cols] = (streams[l].astype(F32) * scale * pgain_ref[:, cols]).astype(BF16)
    for dy in range(4):
        for dz in range(4):
            landed_across(0, dy, dz)

    def encode(i, _):
        cols = pl.ds(pl.multiple_of(i * 256, 256), 256)
        pre = jnp.dot(normed[...], wenc[:, cols], preferred_element_type=F32) + benc_ref[:, cols]
        latents[:, cols] = jnp.maximum(pre, 0.0).astype(BF16)
        return 0

    lax.fori_loop(0, LAT, encode, 0)
    for dy in range(4):
        for dz in range(4):
            landed_across(1, dy, dz)

    def decode(p):
        rows = pl.ds(pl.multiple_of(p * 256, 256), 256)
        return lax.dot_general(
            latents[...], wdec[rows, :], (((1,), (1,)), ((), ())), preferred_element_type=F32
        )

    def decode_step(d, _):
        p = peer_at(d)
        decoded[p] = decode(p).astype(BF16)
        scatter_back(d).start()
        return 0

    lax.fori_loop(1, LAT, decode_step, 0)
    total = decode(me) + streams[me].astype(F32) + bdec_ref[...]
    for d in range(1, LAT):
        p = peer_at(d)
        remote(decoded.at[p], returned.at[p], s3.at[0], r3.at[p], lat=p).wait_recv()
        total = total + returned[p].astype(F32)
    out_ref[...] = total.astype(BF16)
    for d in range(1, LAT):
        scatter(d).wait_send()
        gather(d).wait_send()
        scatter_back(d).wait_send()
    for a in range(2):
        for up in (True, False):
            along_z(a, up).wait_send()
        along_z_on(a).wait_send()
        for dz in range(4):
            for up in (True, False):
                along_y(a, dz, up).wait_send()
            along_y_on(a, dz).wait_send()
            for dy in range(4):
                across(a, dy, dz).wait_send()


def layer(q, k, v, z, bd, wc, gain, residual, pgain, benc, bdec, wout, wenc, wdec):
    vmem = pl.BlockSpec(memory_space=pltpu.VMEM)
    block = pltpu.VMEM((LAT, T, 256), BF16)
    dma = pltpu.SemaphoreType.DMA
    return pl.pallas_call(
        layer_kernel,
        out_shape=jax.ShapeDtypeStruct((T, 256), BF16),
        in_specs=[vmem] * 11 + [pl.BlockSpec(memory_space=pl.ANY)] * 3,
        out_specs=vmem,
        scratch_shapes=[
            pltpu.VMEM((16, 1024), BF16),
            pltpu.VMEM((T + 16, 1024), F32),
            pltpu.VMEM((T, 256), F32),
            pltpu.VMEM((T, 256), F32),
            pltpu.VMEM((T, 512), F32),
            pltpu.VMEM((H, T, W), BF16),
            pltpu.VMEM((H, T, W), F32),
            pltpu.VMEM((H, C, 2 * W), F32),
            pltpu.VMEM((H, 8, W), F32),
            pltpu.VMEM((H, C + 16, 2 * W), BF16),
            pltpu.VMEM((ROW, C + 16, 2 * W), BF16),
            pltpu.VMEM((ROW, C, 2 * W), F32),
            pltpu.VMEM((ROW, 8, W), F32),
            pltpu.VMEM((C + 16, 2 * W), BF16),
            pltpu.VMEM((ROWS, C + 16, 2 * W), BF16),
            pltpu.VMEM((ROW, C, W), BF16),
            pltpu.VMEM((H, C, W), BF16),
            pltpu.VMEM((512, 2048), BF16),
            pltpu.VMEM((2048, 2048), BF16),
            pltpu.VMEM((2048, 2048), BF16),
            block,
            block,
            block,
            pltpu.VMEM((T, 2048), BF16),
            pltpu.VMEM((T, 2048), BF16),
            block,
            block,
            dma((3,)),
            dma((3,)),
            dma((H,)),
            dma((ROW,)),
            dma((ROWS - 1,)),
            dma((ROWS,)),
            dma((ROW,)),
            dma((H,)),
            dma((3,)),
        ]
        + [dma((LAT - 1,)), dma((LAT,))] * 3
        + [dma((2, 16)), dma((2, 16)), dma((2, 16))]
        + [dma((2, 2)), dma((2,)), dma((2, 4, 2)), dma((2, 4))],
        compiler_params=pltpu.CompilerParams(
            collective_id=0, has_side_effects=True, vmem_limit_bytes=VMEM_LIMIT
        ),
        name="layer",
    )(q, k, v, z, bd, wc, gain, residual, pgain, benc, bdec, wout, wenc, wdec)


def per_device(
    q_raw,
    k_raw,
    v_raw,
    z_gate,
    beta_raw,
    decay_log,
    conv_q,
    conv_k,
    conv_v,
    norm_gain,
    w_out,
    residual,
    post_gain,
    w_enc,
    b_enc,
    w_dec,
    b_dec,
):
    bd = jnp.concatenate([beta_raw, decay_log], axis=0)
    bd = bd.reshape(8, T // C, C).transpose(1, 0, 2)
    wc = jnp.concatenate([conv_q, conv_k, conv_v], axis=1)
    return layer(
        q_raw, k_raw, v_raw, z_gate, bd, wc, norm_gain[None, :], residual, post_gain[None, :],
        b_enc[None, :], b_dec[None, :], w_out, w_enc, w_dec,
    )


def solution(mesh):
    return jax.shard_map(
        per_device,
        mesh=mesh,
        in_specs=(
            P("seq", "lat"),
            P("seq", "lat"),
            P("seq", "lat"),
            P("seq", "lat"),
            P("lat", "seq"),
            P("lat", "seq"),
            P(None, "lat"),
            P(None, "lat"),
            P(None, "lat"),
            P(),
            P("lat", None),
            P("seq", "lat"),
            P(),
            P("seq", "lat"),
            P("lat"),
            P("seq", "lat"),
            P("lat"),
        ),
        out_specs=P("seq", "lat"),
        check_vma=False,
    )
```

```python
import functools

import jax
import jax.numpy as jnp
from jax import lax
from jax.experimental import pallas as pl
from jax.experimental.pallas import tpu as pltpu
from jax.sharding import PartitionSpec as P

F32 = jnp.float32
BF16 = jnp.bfloat16
EPSILON = 1e-06
T = 384
C = 128
H = 4
W = 128
ROW = 8
ROWS = 4
LAT = 8
TOP = lax.Precision.HIGHEST
MESH = pl.DeviceIdType.MESH
VMEM_LIMIT = 56 << 20


def mm(a, b, dims=((1,), (0,))):
    return lax.dot_general(
        a.astype(BF16), b.astype(BF16), (dims, ((), ())), preferred_element_type=F32
    )


def halves(a):
    high = a.astype(BF16)
    return high, (a - high.astype(F32)).astype(BF16)


def mm3(a, b, dims=((1,), (0,))):
    ah, al = a
    bh, bl = b
    dot = lambda x, y: lax.dot_general(x, y, (dims, ((), ())), preferred_element_type=F32)
    return dot(ah, bh) + (dot(ah, bl) + dot(al, bh))


def mm6(a, b, dims=((1,), (0,))):
    return lax.dot_general(a, b, (dims, ((), ())), precision=TOP, preferred_element_type=F32)


def silu(v):
    return v / (1.0 + jnp.exp(-v))


def triangular_inverses(systems, row, col):
    first = ((row & 1) == 1) & (col == row - 1)
    eye = (row == col).astype(F32)
    solved = [eye - jnp.where(first, a, 0.0) for a in systems]
    for level in range(1, 7):
        block_row, block_col = row >> level, col >> level
        mask = ((block_row & 1) == 1) & (block_col == block_row - 1)
        parts = [halves(x) for x in solved]
        below = [mm3(halves(jnp.where(mask, a, 0.0)), x) for a, x in zip(systems, parts)]
        solved = [x - mm3(p, halves(b)) for x, p, b in zip(solved, parts, below)]
    return solved


def remote(src, dst, send, recv, **where):
    return pltpu.make_async_remote_copy(
        src_ref=src,
        dst_ref=dst,
        send_sem=send,
        recv_sem=recv,
        device_id=where,
        device_id_type=MESH,
    )


def layer_kernel(
    q_ref, k_ref, v_ref, z_ref, beta_ref, decay_ref, cq_ref, ck_ref, cv_ref, gain_ref,
    res_ref, pgain_ref, benc_ref, bdec_ref, wout_hbm, wenc_hbm, wdec_hbm,
    out_ref,
    bds, halo, pad, qs, ks, vs, ql, ol, comp, acur, msg, slots, prefix, aprefix, tot, tslots, sout, sin,
    wout_ref, wenc, wdec, part, streams, normed, latents, decoded,
    xarr1, zsend1, zrecv1, zarr1, xsend1, xrecv1, xarr2, zsend2, zrecv2, zarr2, xsend2, xrecv2,
    hs, hr, ms, mr, ts, tr, ss, sr,
    wsem, xs1, xr1, zs1, zr1, xs2, xr2, zs2, zr2, gxs, gzs, ga, gr_lat,
    gr, cr, cs, z1s, z2s, y1s, y2s,
):
    seq = lax.axis_index("seq")
    me = lax.axis_index("lat")
    n_seq = ROW * ROWS
    right, left = lax.rem(seq + 1, n_seq), lax.rem(seq + n_seq - 1, n_seq)
    y, j = seq // ROW, lax.rem(seq, ROW)
    zh, core = j // 2, lax.rem(j, 2)
    base = y * ROW

    barrier = pltpu.get_barrier_semaphore()
    pl.semaphore_signal(barrier, inc=1, device_id={"seq": right}, device_id_type=MESH)
    pl.semaphore_signal(barrier, inc=1, device_id={"seq": left}, device_id_type=MESH)
    for d in range(1, ROW):
        peer = base + lax.rem(j + d, ROW)
        pl.semaphore_signal(barrier, inc=1, device_id={"seq": peer}, device_id_type=MESH)
    for d in range(1, ROWS):
        peer = lax.rem(y + d, ROWS) * ROW + j
        pl.semaphore_signal(barrier, inc=1, device_id={"seq": peer}, device_id_type=MESH)
    for d in range(1, LAT):
        peer = lax.rem(me + d, LAT)
        pl.semaphore_signal(barrier, inc=1, device_id={"lat": peer}, device_id_type=MESH)
    pl.semaphore_wait(barrier, 2 + ROW - 1 + ROWS - 1 + LAT - 1)

    full, own_shard = (wenc, wdec), (wenc_hbm, wdec_hbm)
    sibling = base + 2 * zh + 1 - core

    def shard_id(dy, dz):
        return lax.rem(y + dy, ROWS) * 4 + lax.rem(zh + dz, 4)

    def shard(a, s, c, half=None):
        lo, size = (0, 64) if half is None else (32 * half, 32)
        return full[a].at[pl.ds(pl.multiple_of((s * 2 + c) * 64 + lo, 32), size), :]

    def seq_at(dy, dz):
        return shard_id(dy, dz) * 2 + core

    def passed(a, s, sem, to, half=None):
        block = shard(a, s, core, half)
        return remote(block, block, sem, gr.at[a, half or 0, s], seq=to)

    def along_z(a, up):
        s, sem = shard_id(0, 0), z1s.at[a, up]
        return remote(
            own_shard[a], shard(a, s, core), sem, gr.at[a, 0, s], seq=seq_at(0, 1 if up else 3)
        )

    def along_z_on(a, half):
        s, to = (shard_id(0, 3), seq_at(0, 1)) if half == 0 else (shard_id(0, 1), seq_at(0, 3))
        return passed(a, s, z2s.at[a, half], to, half)

    def along_y(a, dz, up):
        s, to, sem = shard_id(0, dz), seq_at(1 if up else 3, 0), y1s.at[a, dz, up]
        if dz == 0:
            return remote(own_shard[a], shard(a, s, core), sem, gr.at[a, 0, s], seq=to)
        return passed(a, s, sem, to)

    def along_y_on(a, dz, half):
        s, to = (shard_id(3, dz), seq_at(1, 0)) if half == 0 else (shard_id(1, dz), seq_at(3, 0))
        return passed(a, s, y2s.at[a, dz, half], to, half)

    def across(a, dy, dz):
        s = shard_id(dy, dz)
        src = own_shard[a] if dy == 0 and dz == 0 else shard(a, s, core)
        return remote(src, shard(a, s, core), cs.at[a, s], cr.at[a, s], seq=sibling)

    def landed(a, dy, dz, half=None):
        s = shard_id(dy, dz)
        passed(a, s, cs.at[a, s], sibling, half).wait_recv()

    def landed_across(a, dy, dz):
        s = shard_id(dy, dz)
        there = shard(a, s, 1 - core)
        remote(there, there, cs.at[a, s], cr.at[a, s], seq=sibling).wait_recv()

    def start_z(a):
        for up in range(2):
            along_z(a, up).start()

    def start_y(a, dz):
        for up in range(2):
            along_y(a, dz, up).start()
        across(a, 0, dz).start()

    def from_z(a):
        for half, dz in enumerate((3, 1)):
            landed(a, 0, dz)
            along_z_on(a, half).start()
        start_y(a, 3)
        start_y(a, 1)

    def from_z_on(a):
        for half in range(2):
            landed(a, 0, 2, half)
        start_y(a, 2)

    def from_y(a, dz):
        for half, dy in enumerate((3, 1)):
            landed(a, dy, dz)
            along_y_on(a, dz, half).start()
            across(a, dy, dz).start()

    def from_y_on(a, dz):
        for half in range(2):
            landed(a, 2, dz, half)
        across(a, 2, dz).start()

    loads = [
        pltpu.make_async_copy(wenc_hbm, shard(0, shard_id(0, 0), core), wsem.at[0]),
        pltpu.make_async_copy(wdec_hbm, shard(1, shard_id(0, 0), core), wsem.at[1]),
        pltpu.make_async_copy(wout_hbm, wout_ref, wsem.at[2]),
    ]
    halos = []
    for i, (ref, lo, width) in enumerate(((q_ref, 0, 256), (k_ref, 256, 256), (v_ref, 512, 512))):
        halos.append(
            remote(
                ref.at[pl.ds(T - 16, 16), :],
                halo.at[:, pl.ds(lo, width)],
                hs.at[i], hr.at[i], seq=right,
            )
        )
        halos[-1].start()
        pad[pl.ds(16, T), lo : lo + width] = ref[...].astype(F32)
    start_z(0)
    start_y(0, 0)
    start_y(1, 0)
    for copy in loads:
        copy.start()
    for copy in halos:
        copy.wait()
    pad[pl.ds(0, 16), :] = jnp.where(seq == 0, 0.0, halo[...].astype(F32))

    bds[0:4, :] = beta_ref[...]
    bds[4:8, :] = decay_ref[...]
    for g in range(8):
        cols = slice(g * W, (g + 1) * W)
        taps = (cq_ref, ck_ref, cv_ref)[min(g // 2, 2)]
        lo = (g - 2 * min(g // 2, 2)) * W
        total = taps[0:1, lo : lo + W] * pad[13 : 13 + T, cols]
        for tap in range(1, 4):
            total = total + taps[tap : tap + 1, lo : lo + W] * pad[13 + tap : 13 + tap + T, cols]
        total = silu(total)
        if g < 4:
            total = total * lax.rsqrt(jnp.sum(total * total, axis=1, keepdims=True) + EPSILON)
        if g < 2:
            qs[:, cols] = total * (W**-0.5)
        elif g < 4:
            ks[:, (g - 2) * W : (g - 1) * W] = total
        else:
            vs[:, (g - 4) * W : (g - 3) * W] = total

    row = lax.broadcasted_iota(jnp.int32, (C, C), 0)
    col = lax.broadcasted_iota(jnp.int32, (C, C), 1)
    lower = (col <= row).astype(F32)
    upper = (row <= col).astype(F32)
    eye = (row == col).astype(F32)
    ones = jnp.ones((C, C), F32)
    comp[...] = jnp.zeros_like(comp)
    acur[...] = jnp.ones_like(acur)

    def block(c, _):
        rows = pl.ds(pl.multiple_of(c * C, C), C)
        bd = bds[:, rows]
        beta_col = mm6(eye, 1.0 / (1.0 + jnp.exp(-bd)), ((1,), (1,)))
        cum_col = mm6(lower, bd, ((1,), (1,)))
        cum_row = mm6(bd, upper)
        tot_row = mm6(bd, ones)
        systems, scores, keys, queries = [], [], [], []
        for kh in range(2):
            k = ks[rows, kh * W : (kh + 1) * W]
            q = qs[rows, kh * W : (kh + 1) * W]
            kp, qp = halves(k), halves(q)
            gram = mm3(kp, kp, ((1,), (1,)))
            score = mm3(qp, kp, ((1,), (1,)))
            keys.append(k)
            queries.append(q)
            for h in (2 * kh, 2 * kh + 1):
                spread = cum_col[:, 4 + h : 5 + h] - cum_row[4 + h : 5 + h, :]
                within = jnp.where(col <= row, jnp.exp(jnp.minimum(spread, 0.0)), 0.0)
                systems.append(
                    jnp.where(col < row, beta_col[:, h : h + 1] * gram * within, 0.0)
                )
                scores.append(score * within)
        solved = triangular_inverses(systems, row, col)
        key_t = [k.T for k in keys]
        for h in range(H):
            kh = h // 2
            beta = beta_col[:, h : h + 1]
            growth = jnp.exp(cum_col[:, 4 + h : 5 + h])
            v = vs[rows, h * W : (h + 1) * W]
            targets = jnp.concatenate([beta * v, (beta * growth) * keys[kh]], axis=1)
            fresh = mm(solved[h], targets).astype(BF16)
            out = mm(scores[h], fresh)
            q_map = growth * queries[kh] - out[:, W:]
            total = tot_row[4 + h : 5 + h, :]
            decay = jnp.exp(total)
            remain = jnp.exp(total - cum_row[4 + h : 5 + h, :])
            new = mm(key_t[kh] * remain, fresh)
            so_far = comp[h]
            a = acur[h, 0:1, :]
            read = mm(q_map, so_far)
            ql[h, rows, :] = (a * q_map - read[:, W:]).astype(BF16)
            ol[h, rows, :] = out[:, :W] + read[:, :W]
            turned = mm(new[:, W:], so_far)
            decay2 = jnp.concatenate([decay, decay], axis=1)
            comp[h] = (
                decay2 * so_far - turned + jnp.concatenate([new[:, :W], a * new[:, W:]], axis=1)
            )
            acur[h] = jnp.broadcast_to(a * decay, (8, W))

        @pl.when(c == 0)
        def _():
            from_z(0)
            start_z(1)

        @pl.when(c == 1)
        def _():
            from_y(0, 0)
            from_y(1, 0)

        return 0

    lax.fori_loop(0, T // C, block, 0)

    def split_row(a):
        high = a.astype(BF16).astype(F32)
        mid = (a - high).astype(BF16).astype(F32)
        low = a - high - mid
        r = lax.broadcasted_iota(jnp.int32, (16, W), 0)
        block = jnp.where(r == 0, high, jnp.where(r == 1, mid, jnp.where(r == 2, low, 0.0)))
        return jnp.concatenate([block, block], axis=1).astype(BF16)

    def joined_row(ref):
        return jnp.sum(ref[C : C + 16, :W].astype(F32), axis=0, keepdims=True)

    for h in range(H):
        msg[h, :C, :] = comp[h].astype(BF16)
        msg[h, C:, :] = split_row(acur[h, 0:1, :])

    def to_handler(h):
        return remote(msg.at[h], slots.at[j], ms.at[h], mr.at[j], seq=base + 2 * h)

    for h in range(H):

        @pl.when(j != 2 * h)
        def _():
            to_handler(h).start()

        @pl.when(j == 2 * h)
        def _():
            slots[j] = msg[h]

    from_z_on(0)

    def total_to(d):
        peer = lax.rem(y + d, ROWS)
        return remote(tot, tslots.at[y], ts.at[d - 1], tr.at[y], seq=peer * ROW + j)

    def state_to(i):
        return remote(sout.at[i], sin.at[zh], ss.at[i], sr.at[zh], seq=base + i)

    @pl.when(core == 0)
    def _():
        for i in range(ROW):

            @pl.when(i != j)
            def _():
                remote(msg.at[0], slots.at[i], ms.at[0], mr.at[i], seq=base + i).wait_recv()

            maps = slots[i, :C, :]
            a_new = joined_row(slots.at[i])
            if i == 0:
                now, a_now = maps.astype(F32), a_new
            else:
                a_old, old = aprefix[i - 1, 0:1, :], prefix[i - 1]
                turned = mm(maps[:, W:], old)
                new = maps.astype(F32)
                a2 = jnp.concatenate([a_new, a_new], axis=1)
                now = (
                    a2 * old - turned + jnp.concatenate([new[:, :W], a_old * new[:, W:]], axis=1)
                )
                a_now = a_old * a_new
            prefix[i] = now
            aprefix[i] = jnp.broadcast_to(a_now, (8, W))
        tot[:C, :] = prefix[ROW - 1].astype(BF16)
        tot[C:, :] = split_row(aprefix[ROW - 1, 0:1, :])
        for d in range(1, ROWS):
            total_to(d).start()
        tslots[y] = tot[...]
        from_z(1)
        state = jnp.zeros((C, W), F32)
        for i in range(ROWS):

            @pl.when(i != y)
            def _():
                remote(tot, tslots.at[i], ts.at[0], tr.at[i], seq=i * ROW + j).wait_recv()

            maps = tslots[i]
            later = (
                joined_row(tslots.at[i]) * state
                - mm(maps[:C, W:], state)
                + maps[:C, :W].astype(F32)
            )
            state = jnp.where(i < y, later, state)
        for i in range(ROW):
            if i == 0:
                mine = state
            else:
                mine = (
                    aprefix[i - 1, 0:1, :] * state
                    - mm(prefix[i - 1, :, W:], state)
                    + prefix[i - 1, :, :W]
                )
            sout[i] = mine.astype(BF16)

            @pl.when(i != j)
            def _():
                state_to(i).start()

            @pl.when(i == j)
            def _():
                sin[zh] = sout[i]

    @pl.when(core == 1)
    def _():
        from_z(1)

    from_y(0, 3)
    from_y(0, 1)
    from_y_on(0, 0)
    from_y_on(1, 0)
    gated = []
    for h in range(H):

        @pl.when(j != 2 * h)
        def _():
            remote(sout.at[0], sin.at[h], ss.at[0], sr.at[h], seq=base + 2 * h).wait_recv()

        delta = ol[h] + mm(ql[h], sin[h])
        squares = jnp.mean(delta * delta, axis=1, keepdims=True)
        gate = silu(z_ref[:, h * W : (h + 1) * W].astype(F32))
        gated.append((delta * lax.rsqrt(squares + EPSILON) * gain_ref[...] * gate).astype(BF16))
    gated = jnp.concatenate(gated, axis=1)
    for copy in loads:
        copy.wait()

    zl, x = me // 4, lax.rem(me, 4)
    other = 1 - zl
    HALF = T // 2

    def lat_at(plane, column):
        return plane * 4 + column

    def column_at(d):
        return lax.rem(x + d, 4)

    def token_rows(block):
        return pl.ds(block * HALF, HALF)

    class ColumnsFirst:
        def __init__(self, src, rows, bufs, sems):
            self.src, self.rows = src, rows
            self.xarr, self.zsend, self.zrecv = bufs
            self.xs, self.xr, self.zs, self.zr = sems

        def to_column(self, d):
            c = column_at(d)
            return remote(
                self.src.at[:, c, self.rows, :], self.xarr.at[:, x],
                self.xs.at[d - 1], self.xr.at[x], lat=lat_at(zl, c),
            )

        def to_plane(self):
            return remote(self.zsend, self.zrecv, self.zs.at[0], self.zr.at[0], lat=lat_at(other, x))

        def turn(self):
            own = self.src[zl, x, self.rows, :].astype(F32)
            theirs = self.src[other, x, self.rows, :].astype(F32)
            for d in range(1, 4):
                c = column_at(d)
                remote(
                    self.src.at[:, c, self.rows, :], self.xarr.at[:, c],
                    self.xs.at[0], self.xr.at[c], lat=lat_at(zl, c),
                ).wait_recv()
                own = own + self.xarr[zl, c].astype(F32)
                theirs = theirs + self.xarr[other, c].astype(F32)
            self.zsend[...] = theirs.astype(BF16)
            self.to_plane().start()
            self.own = own

        def finish(self):
            self.to_plane().wait_recv()
            return self.own + self.zrecv[...].astype(F32)

        def close(self):
            for d in range(1, 4):
                self.to_column(d).wait_send()
            self.to_plane().wait_send()

    class PlanesFirst:
        def __init__(self, src, rows, bufs, sems):
            self.src, self.rows = src, rows
            self.zarr, self.xsend, self.xrecv = bufs
            self.xs, self.xr, self.zs, self.zr = sems

        def to_plane(self):
            return remote(
                self.src.at[other, :, self.rows, :], self.zarr,
                self.zs.at[0], self.zr.at[0], lat=lat_at(other, x),
            )

        def to_column(self, d):
            c = column_at(d)
            return remote(
                self.xsend.at[c], self.xrecv.at[x], self.xs.at[d - 1], self.xr.at[x],
                lat=lat_at(zl, c),
            )

        def turn(self):
            self.to_plane().wait_recv()
            for d in range(1, 4):
                c = column_at(d)
                both = self.src[zl, c, self.rows, :].astype(F32) + self.zarr[c].astype(F32)
                self.xsend[c] = both.astype(BF16)
                self.to_column(d).start()
            self.own = self.src[zl, x, self.rows, :].astype(F32) + self.zarr[x].astype(F32)

        def finish(self):
            total = self.own
            for d in range(1, 4):
                c = column_at(d)
                remote(
                    self.xsend.at[c], self.xrecv.at[c], self.xs.at[0], self.xr.at[c],
                    lat=lat_at(zl, c),
                ).wait_recv()
                total = total + self.xrecv[c].astype(F32)
            return total

        def close(self):
            for d in range(1, 4):
                self.to_column(d).wait_send()
            self.to_plane().wait_send()

    def project(block):
        rows = gated[block * HALF : (block + 1) * HALF, :]
        for lane in range(LAT):
            part[lane // 4, lane % 4, token_rows(block), :] = mm(
                rows, wout_ref[:, lane * 256 : (lane + 1) * 256]
            ).astype(BF16)

    sums1 = (
        ColumnsFirst(part, token_rows(0), (xarr1, zsend1, zrecv1), (xs1.at[0], xr1.at[0], zs1.at[0], zr1.at[0])),
        PlanesFirst(part, token_rows(1), (zarr1, xsend1, xrecv1), (xs1.at[1], xr1.at[1], zs1.at[1], zr1.at[1])),
    )
    sums2 = (
        PlanesFirst(decoded, token_rows(0), (zarr2, xsend2, xrecv2), (xs2.at[0], xr2.at[0], zs2.at[0], zr2.at[0])),
        ColumnsFirst(decoded, token_rows(1), (xarr2, zsend2, zrecv2), (xs2.at[1], xr2.at[1], zs2.at[1], zr2.at[1])),
    )

    def slot(block, plane, column):
        return streams.at[plane, column, token_rows(block), :]

    def give(block, plane, column, sem, **to):
        here = slot(block, plane, column)
        return remote(here, here, sem, gr_lat.at[block, lat_at(plane, column)], **to)

    def give_own_x(block, d):
        return give(block, zl, x, gxs.at[block, d - 1], lat=lat_at(zl, column_at(d)))

    def give_own_z(block):
        return give(block, zl, x, gzs.at[block], lat=lat_at(other, x))

    def give_on(block, d):
        if block == 0:
            return give(0, other, x, ga.at[0, d - 1], lat=lat_at(zl, column_at(d)))
        return give(1, zl, column_at(d), ga.at[1, d - 1], lat=lat_at(other, x))

    def got(block, plane, column):
        give(block, plane, column, gzs.at[block], lat=lat_at(other, x)).wait_recv()

    def enter_stream(block):
        rows = token_rows(block)
        summed = sums1[block].finish()
        streams[zl, x, rows, :] = (res_ref[rows, :].astype(F32) + summed).astype(BF16)
        for d in range(1, 4):
            give_own_x(block, d).start()
        give_own_z(block).start()

    def normalise(block):
        rows = token_rows(block)
        squares = jnp.zeros((HALF, 1), F32)
        for plane in range(2):
            for column in range(4):
                wide = streams[plane, column, rows, :].astype(F32)
                squares = squares + jnp.sum(wide * wide, axis=1, keepdims=True)
        scale = lax.rsqrt(squares * (1.0 / 2048.0) + EPSILON)
        for lane in range(LAT):
            cols = slice(lane * 256, (lane + 1) * 256)
            wide = streams[lane // 4, lane % 4, rows, :].astype(F32)
            normed[rows, cols] = (wide * scale * pgain_ref[:, cols]).astype(BF16)

    def encode(block):
        rows = token_rows(block)

        def step(i, _):
            cols = pl.ds(pl.multiple_of(i * 256, 256), 256)
            pre = jnp.dot(normed[rows, :], wenc[:, cols], preferred_element_type=F32)
            latents[rows, cols] = jnp.maximum(pre + benc_ref[:, cols], 0.0).astype(BF16)
            return 0

        lax.fori_loop(0, LAT, step, 0)

    def decode(block, plane, column):
        rows = token_rows(block)
        features = pl.ds(pl.multiple_of(lat_at(plane, column) * 256, 256), 256)
        decoded[plane, column, rows, :] = lax.dot_general(
            latents[rows, :], wdec[features, :], (((1,), (1,)), ((), ())),
            preferred_element_type=F32,
        ).astype(BF16)

    def leave(block):
        rows = token_rows(block)
        total = sums2[block].finish() + streams[zl, x, rows, :].astype(F32) + bdec_ref[...]
        out_ref[rows, :] = total.astype(BF16)

    project(0)
    for d in range(1, 4):
        sums1[0].to_column(d).start()
    project(1)
    sums1[1].to_plane().start()
    from_z_on(1)
    from_y(0, 2)
    sums1[0].turn()
    sums1[1].turn()
    from_y(1, 3)
    from_y(1, 1)
    enter_stream(0)
    enter_stream(1)
    for dz in range(1, 4):
        from_y_on(0, dz)
    got(0, other, x)
    for d in range(1, 4):
        give_on(0, d).start()
    for d in range(1, 4):
        got(1, zl, column_at(d))
        give_on(1, d).start()
    from_y(1, 2)
    for d in range(1, 4):
        got(0, zl, column_at(d))
    for d in range(1, 4):
        got(0, other, column_at(d))
    normalise(0)
    for dy in range(4):
        for dz in range(4):
            landed_across(0, dy, dz)
    encode(0)
    for dz in range(1, 4):
        from_y_on(1, dz)
    for dy in range(4):
        for dz in range(4):
            landed_across(1, dy, dz)

    def other_plane(i, _):
        decode(0, other, i)
        return 0

    def own_plane(i, _):
        decode(0, zl, i)
        return 0

    lax.fori_loop(0, 4, other_plane, 0)
    sums2[0].to_plane().start()
    lax.fori_loop(0, 4, own_plane, 0)
    for d in range(4):
        got(1, other, column_at(d))
    normalise(1)
    encode(1)
    sums2[0].turn()

    def both_planes(d, _):
        decode(1, 0, column_at(d))
        decode(1, 1, column_at(d))
        return 0

    for d in range(1, 4):
        both_planes(d, 0)
        sums2[1].to_column(d).start()
    both_planes(0, 0)
    leave(0)
    sums2[1].turn()
    leave(1)

    for h in range(H):

        @pl.when(j != 2 * h)
        def _():
            to_handler(h).wait_send()

    @pl.when(core == 0)
    def _():
        for d in range(1, ROWS):
            total_to(d).wait_send()
        for i in range(ROW):

            @pl.when(i != j)
            def _():
                state_to(i).wait_send()

    for sums in sums1 + sums2:
        sums.close()
    for block in range(2):
        for d in range(1, 4):
            give_own_x(block, d).wait_send()
            give_on(block, d).wait_send()
        give_own_z(block).wait_send()
    for a in range(2):
        for side in range(2):
            along_z(a, side).wait_send()
            along_z_on(a, side).wait_send()
        for dz in range(4):
            for side in range(2):
                along_y(a, dz, side).wait_send()
                along_y_on(a, dz, side).wait_send()
            for dy in range(4):
                across(a, dy, dz).wait_send()


def layer(*args):
    vmem = pl.BlockSpec(memory_space=pltpu.VMEM)
    block = pltpu.VMEM((2, 4, T, 256), BF16)
    dma = pltpu.SemaphoreType.DMA
    return pl.pallas_call(
        layer_kernel,
        out_shape=jax.ShapeDtypeStruct((T, 256), BF16),
        in_specs=[vmem] * 14 + [pl.BlockSpec(memory_space=pl.ANY)] * 3,
        out_specs=vmem,
        scratch_shapes=[
            pltpu.VMEM((8, T), F32),
            pltpu.VMEM((16, 1024), BF16),
            pltpu.VMEM((T + 16, 1024), F32),
            pltpu.VMEM((T, 256), F32),
            pltpu.VMEM((T, 256), F32),
            pltpu.VMEM((T, 512), F32),
            pltpu.VMEM((H, T, W), BF16),
            pltpu.VMEM((H, T, W), F32),
            pltpu.VMEM((H, C, 2 * W), F32),
            pltpu.VMEM((H, 8, W), F32),
            pltpu.VMEM((H, C + 16, 2 * W), BF16),
            pltpu.VMEM((ROW, C + 16, 2 * W), BF16),
            pltpu.VMEM((ROW, C, 2 * W), F32),
            pltpu.VMEM((ROW, 8, W), F32),
            pltpu.VMEM((C + 16, 2 * W), BF16),
            pltpu.VMEM((ROWS, C + 16, 2 * W), BF16),
            pltpu.VMEM((ROW, C, W), BF16),
            pltpu.VMEM((H, C, W), BF16),
            pltpu.VMEM((512, 2048), BF16),
            pltpu.VMEM((2048, 2048), BF16),
            pltpu.VMEM((2048, 2048), BF16),
            block,
            block,
            pltpu.VMEM((T, 2048), BF16),
            pltpu.VMEM((T, 2048), BF16),
            block,
        ]
        + [
            pltpu.VMEM((2, 4, T // 2, 256), BF16),
            pltpu.VMEM((T // 2, 256), BF16),
            pltpu.VMEM((T // 2, 256), BF16),
            pltpu.VMEM((4, T // 2, 256), BF16),
            pltpu.VMEM((4, T // 2, 256), BF16),
            pltpu.VMEM((4, T // 2, 256), BF16),
        ]
        * 2
        + [
            dma((3,)),
            dma((3,)),
            dma((H,)),
            dma((ROW,)),
            dma((ROWS - 1,)),
            dma((ROWS,)),
            dma((ROW,)),
            dma((H,)),
            dma((3,)),
        ]
        + [dma((2, 3)), dma((2, 4)), dma((2, 1)), dma((2, 1))] * 2
        + [dma((2, 3)), dma((2,)), dma((2, 3)), dma((2, LAT))]
        + [dma((2, 2, 16)), dma((2, 16)), dma((2, 16))]
        + [dma((2, 2)), dma((2, 2)), dma((2, 4, 2)), dma((2, 4, 2))],
        compiler_params=pltpu.CompilerParams(
            collective_id=0, has_side_effects=True, vmem_limit_bytes=VMEM_LIMIT
        ),
        name="layer",
    )(*args)


def per_device(
    q_raw,
    k_raw,
    v_raw,
    z_gate,
    beta_raw,
    decay_log,
    conv_q,
    conv_k,
    conv_v,
    norm_gain,
    w_out,
    residual,
    post_gain,
    w_enc,
    b_enc,
    w_dec,
    b_dec,
):
    return layer(
        q_raw, k_raw, v_raw, z_gate, beta_raw, decay_log, conv_q, conv_k, conv_v,
        norm_gain[None, :], residual, post_gain[None, :], b_enc[None, :], b_dec[None, :], w_out, w_enc, w_dec,
    )


def solution(mesh):
    return jax.shard_map(
        per_device,
        mesh=mesh,
        in_specs=(
            P("seq", "lat"),
            P("seq", "lat"),
            P("seq", "lat"),
            P("seq", "lat"),
            P("lat", "seq"),
            P("lat", "seq"),
            P(None, "lat"),
            P(None, "lat"),
            P(None, "lat"),
            P(),
            P("lat", None),
            P("seq", "lat"),
            P(),
            P("seq", "lat"),
            P("lat"),
            P("seq", "lat"),
            P("lat"),
        ),
        out_specs=P("seq", "lat"),
        check_vma=False,
    )
```

```python
import functools

import jax
import jax.numpy as jnp
from jax import lax
from jax.experimental import pallas as pl
from jax.experimental.pallas import tpu as pltpu
from jax.sharding import PartitionSpec as P

F32 = jnp.float32
BF16 = jnp.bfloat16
EPSILON = 1e-06
T = 384
C = 128
H = 4
W = 128
ROW = 8
ROWS = 4
LAT = 8
TOP = lax.Precision.HIGHEST
MESH = pl.DeviceIdType.MESH
VMEM_LIMIT = 56 << 20


def mm(a, b, dims=((1,), (0,))):
    return lax.dot_general(
        a.astype(BF16), b.astype(BF16), (dims, ((), ())), preferred_element_type=F32
    )


def halves(a):
    high = a.astype(BF16)
    return high, (a - high.astype(F32)).astype(BF16)


def mm3(a, b, dims=((1,), (0,))):
    ah, al = a
    bh, bl = b
    dot = lambda x, y: lax.dot_general(x, y, (dims, ((), ())), preferred_element_type=F32)
    if dims != ((1,), (0,)):
        return dot(ah, bh) + (dot(ah, bl) + dot(al, bh))
    both = dot(jnp.concatenate([ah, al], axis=1), jnp.concatenate([bh, bh], axis=0))
    return both + dot(ah, bl)


def mm6(a, b, dims=((1,), (0,))):
    return lax.dot_general(a, b, (dims, ((), ())), precision=TOP, preferred_element_type=F32)


def silu(v):
    return v / (1.0 + jnp.exp(-v))


def triangular_inverses(systems, row, col):
    first = ((row & 1) == 1) & (col == row - 1)
    eye = (row == col).astype(F32)
    solved = [eye - jnp.where(first, a, 0.0) for a in systems]
    for level in range(1, 7):
        block_row, block_col = row >> level, col >> level
        mask = ((block_row & 1) == 1) & (block_col == block_row - 1)
        size = 1 << level
        if size < 8:
            parts = [halves(x) for x in solved]
            below = [mm3(halves(jnp.where(mask, a, 0.0)), x) for a, x in zip(systems, parts)]
            solved = [x - mm3(p, halves(b)) for x, p, b in zip(solved, parts, below)]
            continue
        shape = (C // (2 * size), 2, size, C)
        odd = lambda m: m.reshape(shape)[:, 1].reshape(C // 2, C)
        parts = [halves(x) for x in solved]
        below = [mm3(halves(odd(jnp.where(mask, a, 0.0))), x) for a, x in zip(systems, parts)]
        zero = jnp.zeros((C // (2 * size), 1, size, C), F32)
        full = [
            jnp.concatenate([zero, b.reshape(zero.shape)], axis=1).reshape(C, C) for b in below
        ]
        change = [mm3(halves(odd(x)), halves(f)) for x, f in zip(solved, full)]
        solved = [
            x - jnp.concatenate([zero, c.reshape(zero.shape)], axis=1).reshape(C, C)
            for x, c in zip(solved, change)
        ]
    return solved


def remote(src, dst, send, recv, **where):
    return pltpu.make_async_remote_copy(
        src_ref=src,
        dst_ref=dst,
        send_sem=send,
        recv_sem=recv,
        device_id=where,
        device_id_type=MESH,
    )


def layer_kernel(
    q_ref, k_ref, v_ref, z_ref, beta_ref, decay_ref, cq_ref, ck_ref, cv_ref, gain_ref,
    res_ref, pgain_ref, benc_ref, bdec_ref, wout_hbm, wenc_hbm, wdec_hbm,
    out_ref,
    bds, halo, pad, qs, ks, vs, ql, ol, msg, slots, prefix, aprefix, tot, tslots, sout, sin,
    wout_ref, wenc, wdec, part, streams, normed, latents, decoded,
    xarr1, zsend1, zrecv1, zarr1, xsend1, xrecv1, xarr2, zsend2, zrecv2, zarr2, xsend2, xrecv2,
    hs, hr, ms, mr, ts, tr, ss, sr,
    wsem, xs1, xr1, zs1, zr1, xs2, xr2, zs2, zr2, gxs, gzs, ga, gr_lat,
    gr, cr, cs, z1s, z2s, y1s, y2s,
):
    seq = lax.axis_index("seq")
    me = lax.axis_index("lat")
    n_seq = ROW * ROWS
    right, left = lax.rem(seq + 1, n_seq), lax.rem(seq + n_seq - 1, n_seq)
    y, j = seq // ROW, lax.rem(seq, ROW)
    zh, core = j // 2, lax.rem(j, 2)
    base = y * ROW

    barrier = pltpu.get_barrier_semaphore()
    pl.semaphore_signal(barrier, inc=1, device_id={"seq": right}, device_id_type=MESH)
    pl.semaphore_signal(barrier, inc=1, device_id={"seq": left}, device_id_type=MESH)
    for d in range(1, ROW):
        peer = base + lax.rem(j + d, ROW)
        pl.semaphore_signal(barrier, inc=1, device_id={"seq": peer}, device_id_type=MESH)
    for d in range(1, ROWS):
        peer = lax.rem(y + d, ROWS) * ROW + j
        pl.semaphore_signal(barrier, inc=1, device_id={"seq": peer}, device_id_type=MESH)
    for d in range(1, LAT):
        peer = lax.rem(me + d, LAT)
        pl.semaphore_signal(barrier, inc=1, device_id={"lat": peer}, device_id_type=MESH)
    pl.semaphore_wait(barrier, 2 + ROW - 1 + ROWS - 1 + LAT - 1)

    full, own_shard = (wenc, wdec), (wenc_hbm, wdec_hbm)
    sibling = base + 2 * zh + 1 - core

    def shard_id(dy, dz):
        return lax.rem(y + dy, ROWS) * 4 + lax.rem(zh + dz, 4)

    def shard(a, s, c, half=None):
        if half is None:
            return full[a].at[s, c]
        return full[a].at[s, c, pl.ds(32 * half, 32), :]

    def slab(a, dy, c):
        return full[a].at[pl.ds(lax.rem(y + dy, ROWS) * 4, 4), c]

    def seq_at(dy, dz):
        return shard_id(dy, dz) * 2 + core

    def passed(a, s, sem, to, half=None):
        block = shard(a, s, core, half)
        return remote(block, block, sem, gr.at[a, half or 0, s], seq=to)

    def along_z(a, up):
        s, sem = shard_id(0, 0), z1s.at[a, up]
        return remote(
            own_shard[a], shard(a, s, core), sem, gr.at[a, 0, s], seq=seq_at(0, 1 if up else 3)
        )

    def along_z_on(a, half):
        s, to = (shard_id(0, 3), seq_at(0, 1)) if half == 0 else (shard_id(0, 1), seq_at(0, 3))
        return passed(a, s, z2s.at[a, half], to, half)

    def along_y(a, dz, up):
        s, to, sem = shard_id(0, dz), seq_at(1 if up else 3, 0), y1s.at[a, dz, up]
        if dz == 0:
            return remote(own_shard[a], shard(a, s, core), sem, gr.at[a, 0, s], seq=to)
        return passed(a, s, sem, to)

    def along_y_on(a, dz, half):
        s, to = (shard_id(3, dz), seq_at(1, 0)) if half == 0 else (shard_id(1, dz), seq_at(3, 0))
        return passed(a, s, y2s.at[a, dz, half], to, half)

    def across(a, dy):
        block = slab(a, dy, core)
        return remote(block, block, cs.at[a, dy], cr.at[a, dy], seq=sibling)

    def landed(a, dy, dz, half=None):
        s = shard_id(dy, dz)
        passed(a, s, cs.at[a, 0], sibling, half).wait_recv()

    def landed_across(a):
        for dy in range(ROWS):
            block = slab(a, dy, 1 - core)
            remote(block, block, cs.at[a, dy], cr.at[a, dy], seq=sibling).wait_recv()

    def start_z(a):
        for up in range(2):
            along_z(a, up).start()

    def start_y(a, dz):
        for up in range(2):
            along_y(a, dz, up).start()

    def from_z(a):
        for half, dz in enumerate((3, 1)):
            landed(a, 0, dz)
            along_z_on(a, half).start()
        start_y(a, 3)
        start_y(a, 1)

    def from_z_on(a):
        for half in range(2):
            landed(a, 0, 2, half)
        start_y(a, 2)
        loads[a].wait()
        across(a, 0).start()

    def from_y(a, dz):
        for half, dy in enumerate((3, 1)):
            landed(a, dy, dz)
            along_y_on(a, dz, half).start()
            if dz == 2:
                across(a, dy).start()

    def from_y_on(a):
        for dz in range(4):
            for half in range(2):
                landed(a, 2, dz, half)
        across(a, 2).start()

    loads = [
        pltpu.make_async_copy(wenc_hbm, shard(0, shard_id(0, 0), core), wsem.at[0]),
        pltpu.make_async_copy(wdec_hbm, shard(1, shard_id(0, 0), core), wsem.at[1]),
        pltpu.make_async_copy(wout_hbm, wout_ref, wsem.at[2]),
    ]
    halos = []
    for i, (ref, lo, width) in enumerate(((q_ref, 0, 256), (k_ref, 256, 256), (v_ref, 512, 512))):
        halos.append(
            remote(
                ref.at[pl.ds(T - 16, 16), :],
                halo.at[:, pl.ds(lo, width)],
                hs.at[i], hr.at[i], seq=right,
            )
        )
        halos[-1].start()
        pad[pl.ds(16, T), lo : lo + width] = ref[...].astype(F32)
    start_z(0)
    start_y(0, 0)
    start_y(1, 0)
    for copy in loads:
        copy.start()
    for copy in halos:
        copy.wait()
    pad[pl.ds(0, 16), :] = jnp.where(seq == 0, 0.0, halo[...].astype(F32))

    bds[0:4, :] = beta_ref[...]
    bds[4:8, :] = decay_ref[...]
    for g in range(8):
        cols = slice(g * W, (g + 1) * W)
        taps = (cq_ref, ck_ref, cv_ref)[min(g // 2, 2)]
        lo = (g - 2 * min(g // 2, 2)) * W
        total = taps[0:1, lo : lo + W] * pad[13 : 13 + T, cols]
        for tap in range(1, 4):
            total = total + taps[tap : tap + 1, lo : lo + W] * pad[13 + tap : 13 + tap + T, cols]
        total = silu(total)
        if g < 4:
            total = total * lax.rsqrt(jnp.sum(total * total, axis=1, keepdims=True) + EPSILON)
        if g < 2:
            qs[:, cols] = total * (W**-0.5)
        elif g < 4:
            ks[:, (g - 2) * W : (g - 1) * W] = total
        else:
            vs[:, (g - 4) * W : (g - 3) * W] = total

    row = lax.broadcasted_iota(jnp.int32, (C, C), 0)
    col = lax.broadcasted_iota(jnp.int32, (C, C), 1)
    lower = (col <= row).astype(F32)
    upper = (row <= col).astype(F32)
    eye = (row == col).astype(F32)
    ones = jnp.ones((C, C), F32)

    systems, scores, keys, queries, cums = [], [], [], [], []
    for c in range(T // C):
        rows = slice(c * C, (c + 1) * C)
        bd = bds[:, rows]
        beta_col = mm6(eye, 1.0 / (1.0 + jnp.exp(-bd)), ((1,), (1,)))
        cum_col = mm6(lower, bd, ((1,), (1,)))
        cum_row = mm6(bd, upper)
        cums.append((beta_col, cum_col, cum_row, mm6(bd, ones)))
        for kh in range(2):
            k = ks[rows, kh * W : (kh + 1) * W]
            q = qs[rows, kh * W : (kh + 1) * W]
            kp, qp = halves(k), halves(q)
            gram = mm3(kp, kp, ((1,), (1,)))
            score = mm3(qp, kp, ((1,), (1,)))
            keys.append(k)
            queries.append(q)
            for h in (2 * kh, 2 * kh + 1):
                spread = cum_col[:, 4 + h : 5 + h] - cum_row[4 + h : 5 + h, :]
                within = jnp.where(col <= row, jnp.exp(jnp.minimum(spread, 0.0)), 0.0)
                systems.append(
                    jnp.where(col < row, beta_col[:, h : h + 1] * gram * within, 0.0)
                )
                scores.append((score * within).astype(BF16))
    solved = [x.astype(BF16) for x in triangular_inverses(systems, row, col)]
    from_z(0)
    start_z(1)

    key_t = [k.T for k in keys]
    every = [(c, h) for c in range(T // C) for h in range(H)]
    fresh, out, new = [], [], []
    for i, (c, h) in enumerate(every):
        beta_col, cum_col, _, _ = cums[c]
        beta = beta_col[:, h : h + 1]
        growth = jnp.exp(cum_col[:, 4 + h : 5 + h])
        v = vs[c * C : (c + 1) * C, h * W : (h + 1) * W]
        k = keys[2 * c + h // 2]
        targets = jnp.concatenate([beta * v, (beta * growth) * k], axis=1)
        fresh.append(mm(solved[i], targets).astype(BF16))
    for i, (c, h) in enumerate(every):
        _, _, cum_row, tot_row = cums[c]
        remain = jnp.exp(tot_row[4 + h : 5 + h, :] - cum_row[4 + h : 5 + h, :])
        out.append(mm(scores[i], fresh[i]))
        new.append(mm(key_t[2 * c + h // 2] * remain, fresh[i]))
    from_y(0, 0)
    from_y(1, 0)
    comp, acur = [None] * H, [None] * H
    for i, (c, h) in enumerate(every):
        _, cum_col, _, tot_row = cums[c]
        rows = slice(c * C, (c + 1) * C)
        q_map = jnp.exp(cum_col[:, 4 + h : 5 + h]) * queries[2 * c + h // 2] - out[i][:, W:]
        decay = jnp.exp(tot_row[4 + h : 5 + h, :])
        if c == 0:
            ql[h, rows, :] = q_map.astype(BF16)
            ol[h, rows, :] = out[i][:, :W]
            comp[h], acur[h] = new[i], decay
            continue
        a, so_far = acur[h], comp[h]
        read = mm(q_map, so_far)
        ql[h, rows, :] = (a * q_map - read[:, W:]).astype(BF16)
        ol[h, rows, :] = out[i][:, :W] + read[:, :W]
        turned = mm(new[i][:, W:], so_far)
        comp[h] = (
            jnp.concatenate([decay, decay], axis=1) * so_far
            - turned
            + jnp.concatenate([new[i][:, :W], a * new[i][:, W:]], axis=1)
        )
        acur[h] = a * decay

    def split_row(a):
        high = a.astype(BF16).astype(F32)
        mid = (a - high).astype(BF16).astype(F32)
        low = a - high - mid
        r = lax.broadcasted_iota(jnp.int32, (16, W), 0)
        block = jnp.where(r == 0, high, jnp.where(r == 1, mid, jnp.where(r == 2, low, 0.0)))
        return jnp.concatenate([block, block], axis=1).astype(BF16)

    def joined_row(ref):
        return jnp.sum(ref[C : C + 16, :W].astype(F32), axis=0, keepdims=True)

    for h in range(H):
        msg[h, :C, :] = comp[h].astype(BF16)
        msg[h, C:, :] = split_row(acur[h])

    def to_handler(h):
        return remote(msg.at[h], slots.at[j], ms.at[h], mr.at[j], seq=base + 2 * h)

    for h in range(H):

        @pl.when(j != 2 * h)
        def _():
            to_handler(h).start()

        @pl.when(j == 2 * h)
        def _():
            slots[j] = msg[h]

    def total_to(d):
        peer = lax.rem(y + d, ROWS)
        return remote(tot, tslots.at[y], ts.at[d - 1], tr.at[y], seq=peer * ROW + j)

    def state_to(i):
        return remote(sout.at[i], sin.at[zh], ss.at[i], sr.at[zh], seq=base + i)

    @pl.when(core == 0)
    def _():
        for i in range(ROW):

            @pl.when(i != j)
            def _():
                remote(msg.at[0], slots.at[i], ms.at[0], mr.at[i], seq=base + i).wait_recv()

            maps = slots[i, :C, :]
            a_new = joined_row(slots.at[i])
            if i == 0:
                now, a_now = maps.astype(F32), a_new
            else:
                a_old, old = aprefix[i - 1, 0:1, :], prefix[i - 1]
                turned = mm(maps[:, W:], old)
                new = maps.astype(F32)
                a2 = jnp.concatenate([a_new, a_new], axis=1)
                now = (
                    a2 * old - turned + jnp.concatenate([new[:, :W], a_old * new[:, W:]], axis=1)
                )
                a_now = a_old * a_new
            prefix[i] = now
            aprefix[i] = jnp.broadcast_to(a_now, (8, W))
        tot[:C, :] = prefix[ROW - 1].astype(BF16)
        tot[C:, :] = split_row(aprefix[ROW - 1, 0:1, :])
        for d in range(1, ROWS):
            total_to(d).start()
        tslots[y] = tot[...]
        from_z_on(0)
        from_z(1)
        state = jnp.zeros((C, W), F32)
        for i in range(ROWS):

            @pl.when(i != y)
            def _():
                remote(tot, tslots.at[i], ts.at[0], tr.at[i], seq=i * ROW + j).wait_recv()

            maps = tslots[i]
            later = (
                joined_row(tslots.at[i]) * state
                - mm(maps[:C, W:], state)
                + maps[:C, :W].astype(F32)
            )
            state = jnp.where(i < y, later, state)
        for i in range(ROW):
            if i == 0:
                mine = state
            else:
                mine = (
                    aprefix[i - 1, 0:1, :] * state
                    - mm(prefix[i - 1, :, W:], state)
                    + prefix[i - 1, :, :W]
                )
            sout[i] = mine.astype(BF16)

            @pl.when(i != j)
            def _():
                state_to(i).start()

            @pl.when(i == j)
            def _():
                sin[zh] = sout[i]

    @pl.when(core == 1)
    def _():
        from_z_on(0)
        from_z(1)

    from_y(0, 3)
    from_y(0, 1)
    gated = []
    for h in range(H):

        @pl.when(j != 2 * h)
        def _():
            remote(sout.at[0], sin.at[h], ss.at[0], sr.at[h], seq=base + 2 * h).wait_recv()

        delta = ol[h] + mm(ql[h], sin[h])
        squares = jnp.mean(delta * delta, axis=1, keepdims=True)
        gate = silu(z_ref[:, h * W : (h + 1) * W].astype(F32))
        gated.append((delta * lax.rsqrt(squares + EPSILON) * gain_ref[...] * gate).astype(BF16))
    gated = jnp.concatenate(gated, axis=1)
    loads[2].wait()

    zl, x = me // 4, lax.rem(me, 4)
    other = 1 - zl
    HALF = T // 2

    def lat_at(plane, column):
        return plane * 4 + column

    def column_at(d):
        return lax.rem(x + d, 4)

    def token_rows(block):
        return pl.ds(block * HALF, HALF)

    class ColumnsFirst:
        def __init__(self, src, rows, bufs, sems):
            self.src, self.rows = src, rows
            self.xarr, self.zsend, self.zrecv = bufs
            self.xs, self.xr, self.zs, self.zr = sems

        def to_column(self, d):
            c = column_at(d)
            return remote(
                self.src.at[:, c, self.rows, :], self.xarr.at[:, x],
                self.xs.at[d - 1], self.xr.at[x], lat=lat_at(zl, c),
            )

        def to_plane(self):
            return remote(self.zsend, self.zrecv, self.zs.at[0], self.zr.at[0], lat=lat_at(other, x))

        def turn(self):
            own = self.src[zl, x, self.rows, :].astype(F32)
            theirs = self.src[other, x, self.rows, :].astype(F32)
            for d in range(1, 4):
                c = column_at(d)
                remote(
                    self.src.at[:, c, self.rows, :], self.xarr.at[:, c],
                    self.xs.at[0], self.xr.at[c], lat=lat_at(zl, c),
                ).wait_recv()
                own = own + self.xarr[zl, c].astype(F32)
                theirs = theirs + self.xarr[other, c].astype(F32)
            self.zsend[...] = theirs.astype(BF16)
            self.to_plane().start()
            self.own = own

        def finish(self):
            self.to_plane().wait_recv()
            return self.own + self.zrecv[...].astype(F32)

        def close(self):
            for d in range(1, 4):
                self.to_column(d).wait_send()
            self.to_plane().wait_send()

    class PlanesFirst:
        def __init__(self, src, rows, bufs, sems):
            self.src, self.rows = src, rows
            self.zarr, self.xsend, self.xrecv = bufs
            self.xs, self.xr, self.zs, self.zr = sems

        def to_plane(self):
            return remote(
                self.src.at[other, :, self.rows, :], self.zarr,
                self.zs.at[0], self.zr.at[0], lat=lat_at(other, x),
            )

        def to_column(self, d):
            c = column_at(d)
            return remote(
                self.xsend.at[c], self.xrecv.at[x], self.xs.at[d - 1], self.xr.at[x],
                lat=lat_at(zl, c),
            )

        def turn(self):
            self.to_plane().wait_recv()
            for d in range(1, 4):
                c = column_at(d)
                both = self.src[zl, c, self.rows, :].astype(F32) + self.zarr[c].astype(F32)
                self.xsend[c] = both.astype(BF16)
                self.to_column(d).start()
            self.own = self.src[zl, x, self.rows, :].astype(F32) + self.zarr[x].astype(F32)

        def finish(self):
            total = self.own
            for d in range(1, 4):
                c = column_at(d)
                remote(
                    self.xsend.at[c], self.xrecv.at[c], self.xs.at[0], self.xr.at[c],
                    lat=lat_at(zl, c),
                ).wait_recv()
                total = total + self.xrecv[c].astype(F32)
            return total

        def close(self):
            for d in range(1, 4):
                self.to_column(d).wait_send()
            self.to_plane().wait_send()

    def project(block):
        rows = gated[block * HALF : (block + 1) * HALF, :]
        for lane in range(LAT):
            part[lane // 4, lane % 4, token_rows(block), :] = mm(
                rows, wout_ref[:, lane * 256 : (lane + 1) * 256]
            ).astype(BF16)

    sums1 = (
        ColumnsFirst(part, token_rows(0), (xarr1, zsend1, zrecv1), (xs1.at[0], xr1.at[0], zs1.at[0], zr1.at[0])),
        PlanesFirst(part, token_rows(1), (zarr1, xsend1, xrecv1), (xs1.at[1], xr1.at[1], zs1.at[1], zr1.at[1])),
    )
    sums2 = (
        PlanesFirst(decoded, token_rows(0), (zarr2, xsend2, xrecv2), (xs2.at[0], xr2.at[0], zs2.at[0], zr2.at[0])),
        ColumnsFirst(decoded, token_rows(1), (xarr2, zsend2, zrecv2), (xs2.at[1], xr2.at[1], zs2.at[1], zr2.at[1])),
    )

    def slot(block, plane, column):
        return streams.at[plane, column, token_rows(block), :]

    def give(block, plane, column, sem, **to):
        here = slot(block, plane, column)
        return remote(here, here, sem, gr_lat.at[block, lat_at(plane, column)], **to)

    def give_own_x(block, d):
        return give(block, zl, x, gxs.at[block, d - 1], lat=lat_at(zl, column_at(d)))

    def give_own_z(block):
        return give(block, zl, x, gzs.at[block], lat=lat_at(other, x))

    def give_on(block, d):
        if block == 0:
            return give(0, other, x, ga.at[0, d - 1], lat=lat_at(zl, column_at(d)))
        return give(1, zl, column_at(d), ga.at[1, d - 1], lat=lat_at(other, x))

    def got(block, plane, column):
        give(block, plane, column, gzs.at[block], lat=lat_at(other, x)).wait_recv()

    def enter_stream(block):
        rows = token_rows(block)
        summed = sums1[block].finish()
        streams[zl, x, rows, :] = (res_ref[rows, :].astype(F32) + summed).astype(BF16)
        for d in range(1, 4):
            give_own_x(block, d).start()
        give_own_z(block).start()

    def normalise(block):
        rows = token_rows(block)
        squares = jnp.zeros((HALF, 1), F32)
        for plane in range(2):
            for column in range(4):
                wide = streams[plane, column, rows, :].astype(F32)
                squares = squares + jnp.sum(wide * wide, axis=1, keepdims=True)
        scale = lax.rsqrt(squares * (1.0 / 2048.0) + EPSILON)
        for lane in range(LAT):
            cols = slice(lane * 256, (lane + 1) * 256)
            wide = streams[lane // 4, lane % 4, rows, :].astype(F32)
            normed[rows, cols] = (wide * scale * pgain_ref[:, cols]).astype(BF16)

    def encode(block):
        rows = token_rows(block)

        def step(i, _):
            cols = pl.ds(pl.multiple_of(i * 256, 256), 256)
            features = wenc[:, :, :, cols].reshape(2048, 256)
            pre = jnp.dot(normed[rows, :], features, preferred_element_type=F32)
            latents[rows, cols] = jnp.maximum(pre + benc_ref[:, cols], 0.0).astype(BF16)
            return 0

        lax.fori_loop(0, LAT, step, 0)

    def decode(plane, column):
        rows = wdec[pl.ds(lat_at(plane, column) * 2, 2)].reshape(256, 2048)
        decoded[plane, column] = lax.dot_general(
            latents[...], rows, (((1,), (1,)), ((), ())), preferred_element_type=F32
        ).astype(BF16)

    def leave(block):
        rows = token_rows(block)
        total = sums2[block].finish() + streams[zl, x, rows, :].astype(F32) + bdec_ref[...]
        out_ref[rows, :] = total.astype(BF16)

    project(0)
    for d in range(1, 4):
        sums1[0].to_column(d).start()
    project(1)
    sums1[1].to_plane().start()
    from_z_on(1)
    from_y(0, 2)
    sums1[0].turn()
    sums1[1].turn()
    from_y(1, 3)
    from_y(1, 1)
    enter_stream(0)
    enter_stream(1)
    from_y_on(0)
    got(0, other, x)
    for d in range(1, 4):
        give_on(0, d).start()
    for d in range(1, 4):
        got(1, zl, column_at(d))
        give_on(1, d).start()
    from_y(1, 2)
    for d in range(1, 4):
        got(0, zl, column_at(d))
    for d in range(1, 4):
        got(0, other, column_at(d))
    normalise(0)
    landed_across(0)
    encode(0)
    from_y_on(1)
    for d in range(4):
        got(1, other, column_at(d))
    normalise(1)
    encode(1)
    landed_across(1)

    def other_plane(i, _):
        decode(other, i)
        return 0

    lax.fori_loop(0, 4, other_plane, 0)
    sums2[0].to_plane().start()

    def own_plane(d, _):
        decode(zl, column_at(d))
        sums2[1].to_column(d).start()
        return 0

    lax.fori_loop(1, 4, own_plane, 0)
    decode(zl, x)

    for h in range(H):

        @pl.when(j != 2 * h)
        def _():
            to_handler(h).wait_send()

    @pl.when(core == 0)
    def _():
        for d in range(1, ROWS):
            total_to(d).wait_send()
        for i in range(ROW):

            @pl.when(i != j)
            def _():
                state_to(i).wait_send()

    for sums in sums1:
        sums.close()
    for block in range(2):
        for d in range(1, 4):
            give_own_x(block, d).wait_send()
            give_on(block, d).wait_send()
        give_own_z(block).wait_send()
    for a in range(2):
        for side in range(2):
            along_z(a, side).wait_send()
            along_z_on(a, side).wait_send()
        for dz in range(4):
            for side in range(2):
                along_y(a, dz, side).wait_send()
                along_y_on(a, dz, side).wait_send()
        for dy in range(ROWS):
            across(a, dy).wait_send()
    sums2[0].turn()
    sums2[1].turn()
    leave(0)
    leave(1)
    for sums in sums2:
        sums.close()


def layer(*args):
    vmem = pl.BlockSpec(memory_space=pltpu.VMEM)
    block = pltpu.VMEM((2, 4, T, 256), BF16)
    dma = pltpu.SemaphoreType.DMA
    return pl.pallas_call(
        layer_kernel,
        out_shape=jax.ShapeDtypeStruct((T, 256), BF16),
        in_specs=[vmem] * 14 + [pl.BlockSpec(memory_space=pl.ANY)] * 3,
        out_specs=vmem,
        scratch_shapes=[
            pltpu.VMEM((8, T), F32),
            pltpu.VMEM((16, 1024), BF16),
            pltpu.VMEM((T + 16, 1024), F32),
            pltpu.VMEM((T, 256), F32),
            pltpu.VMEM((T, 256), F32),
            pltpu.VMEM((T, 512), F32),
            pltpu.VMEM((H, T, W), BF16),
            pltpu.VMEM((H, T, W), F32),
            pltpu.VMEM((H, C + 16, 2 * W), BF16),
            pltpu.VMEM((ROW, C + 16, 2 * W), BF16),
            pltpu.VMEM((ROW, C, 2 * W), F32),
            pltpu.VMEM((ROW, 8, W), F32),
            pltpu.VMEM((C + 16, 2 * W), BF16),
            pltpu.VMEM((ROWS, C + 16, 2 * W), BF16),
            pltpu.VMEM((ROW, C, W), BF16),
            pltpu.VMEM((H, C, W), BF16),
            pltpu.VMEM((512, 2048), BF16),
            pltpu.VMEM((16, 2, 64, 2048), BF16),
            pltpu.VMEM((16, 2, 64, 2048), BF16),
            block,
            block,
            pltpu.VMEM((T, 2048), BF16),
            pltpu.VMEM((T, 2048), BF16),
            block,
        ]
        + [
            pltpu.VMEM((2, 4, T // 2, 256), BF16),
            pltpu.VMEM((T // 2, 256), BF16),
            pltpu.VMEM((T // 2, 256), BF16),
            pltpu.VMEM((4, T // 2, 256), BF16),
            pltpu.VMEM((4, T // 2, 256), BF16),
            pltpu.VMEM((4, T // 2, 256), BF16),
        ]
        * 2
        + [
            dma((3,)),
            dma((3,)),
            dma((H,)),
            dma((ROW,)),
            dma((ROWS - 1,)),
            dma((ROWS,)),
            dma((ROW,)),
            dma((H,)),
            dma((3,)),
        ]
        + [dma((2, 3)), dma((2, 4)), dma((2, 1)), dma((2, 1))] * 2
        + [dma((2, 3)), dma((2,)), dma((2, 3)), dma((2, LAT))]
        + [dma((2, 2, 16)), dma((2, 4)), dma((2, 4))]
        + [dma((2, 2)), dma((2, 2)), dma((2, 4, 2)), dma((2, 4, 2))],
        compiler_params=pltpu.CompilerParams(
            collective_id=0, has_side_effects=True, vmem_limit_bytes=VMEM_LIMIT
        ),
        name="layer",
    )(*args)


def per_device(
    q_raw,
    k_raw,
    v_raw,
    z_gate,
    beta_raw,
    decay_log,
    conv_q,
    conv_k,
    conv_v,
    norm_gain,
    w_out,
    residual,
    post_gain,
    w_enc,
    b_enc,
    w_dec,
    b_dec,
):
    return layer(
        q_raw, k_raw, v_raw, z_gate, beta_raw, decay_log, conv_q, conv_k, conv_v,
        norm_gain[None, :], residual, post_gain[None, :], b_enc[None, :], b_dec[None, :], w_out, w_enc, w_dec,
    )


def solution(mesh):
    return jax.shard_map(
        per_device,
        mesh=mesh,
        in_specs=(
            P("seq", "lat"),
            P("seq", "lat"),
            P("seq", "lat"),
            P("seq", "lat"),
            P("lat", "seq"),
            P("lat", "seq"),
            P(None, "lat"),
            P(None, "lat"),
            P(None, "lat"),
            P(),
            P("lat", None),
            P("seq", "lat"),
            P(),
            P("seq", "lat"),
            P("lat"),
            P("seq", "lat"),
            P("lat"),
        ),
        out_specs=P("seq", "lat"),
        check_vma=False,
    )
```

```python
import functools

import jax
import jax.numpy as jnp
from jax import lax
from jax.experimental import pallas as pl
from jax.experimental.pallas import tpu as pltpu
from jax.sharding import PartitionSpec as P

F32 = jnp.float32
BF16 = jnp.bfloat16
EPSILON = 1e-06
T = 384
C = 128
H = 4
W = 128
ROW = 8
ROWS = 4
LAT = 8
TOP = lax.Precision.HIGHEST
MESH = pl.DeviceIdType.MESH
VMEM_LIMIT = 56 << 20


def mm(a, b, dims=((1,), (0,))):
    return lax.dot_general(
        a.astype(BF16), b.astype(BF16), (dims, ((), ())), preferred_element_type=F32
    )


def halves(a):
    high = a.astype(BF16)
    return high, (a - high.astype(F32)).astype(BF16)


def mm3(a, b, dims=((1,), (0,))):
    ah, al = a
    bh, bl = b
    dot = lambda x, y: lax.dot_general(x, y, (dims, ((), ())), preferred_element_type=F32)
    if dims != ((1,), (0,)):
        return dot(ah, bh) + (dot(ah, bl) + dot(al, bh))
    both = dot(jnp.concatenate([ah, al], axis=1), jnp.concatenate([bh, bh], axis=0))
    return both + dot(ah, bl)


def mm6(a, b, dims=((1,), (0,))):
    return lax.dot_general(a, b, (dims, ((), ())), precision=TOP, preferred_element_type=F32)


def silu(v):
    return v / (1.0 + jnp.exp(-v))


def triangular_inverses(systems, row, col):
    first = ((row & 1) == 1) & (col == row - 1)
    eye = (row == col).astype(F32)
    solved = [eye - jnp.where(first, a, 0.0) for a in systems]
    for level in range(1, 7):
        block_row, block_col = row >> level, col >> level
        mask = ((block_row & 1) == 1) & (block_col == block_row - 1)
        size = 1 << level
        if size < 8:
            parts = [halves(x) for x in solved]
            below = [mm3(halves(jnp.where(mask, a, 0.0)), x) for a, x in zip(systems, parts)]
            solved = [x - mm3(p, halves(b)) for x, p, b in zip(solved, parts, below)]
            continue
        shape = (C // (2 * size), 2, size, C)
        odd = lambda m: m.reshape(shape)[:, 1].reshape(C // 2, C)
        parts = [halves(x) for x in solved]
        below = [mm3(halves(odd(jnp.where(mask, a, 0.0))), x) for a, x in zip(systems, parts)]
        zero = jnp.zeros((C // (2 * size), 1, size, C), F32)
        full = [
            jnp.concatenate([zero, b.reshape(zero.shape)], axis=1).reshape(C, C) for b in below
        ]
        change = [mm3(halves(odd(x)), halves(f)) for x, f in zip(solved, full)]
        solved = [
            x - jnp.concatenate([zero, c.reshape(zero.shape)], axis=1).reshape(C, C)
            for x, c in zip(solved, change)
        ]
    return solved


def remote(src, dst, send, recv, **where):
    return pltpu.make_async_remote_copy(
        src_ref=src,
        dst_ref=dst,
        send_sem=send,
        recv_sem=recv,
        device_id=where,
        device_id_type=MESH,
    )


def layer_kernel(
    q_ref, k_ref, v_ref, z_ref, beta_ref, decay_ref, cq_ref, ck_ref, cv_ref, gain_ref,
    res_ref, pgain_ref, benc_ref, bdec_ref, wout_hbm, wenc_hbm, wdec_hbm,
    out_ref,
    bds, halo, pad, qs, ks, vs, ql, ol, msg, slots, prefix, aprefix, tot, tslots, sout, sin,
    wout_ref, wenc, wdec, part, streams, normed, latents, decoded,
    xarr1, zsend1, zrecv1, zarr1, xsend1, xrecv1, xarr2, zsend2, zrecv2, zarr2, xsend2, xrecv2,
    hs, hr, ms, mr, ts, tr, ss, sr,
    wsem, xs1, xr1, zs1, zr1, xs2, xr2, zs2, zr2, gxs, gzs, ga, gr_lat,
    gr, cr, cs, z1s, z2s, y1s, y2s,
):
    seq = lax.axis_index("seq")
    me = lax.axis_index("lat")
    n_seq = ROW * ROWS
    right, left = lax.rem(seq + 1, n_seq), lax.rem(seq + n_seq - 1, n_seq)
    y, j = seq // ROW, lax.rem(seq, ROW)
    zh, core = j // 2, lax.rem(j, 2)
    base = y * ROW

    barrier = pltpu.get_barrier_semaphore()
    pl.semaphore_signal(barrier, inc=1, device_id={"seq": right}, device_id_type=MESH)
    pl.semaphore_signal(barrier, inc=1, device_id={"seq": left}, device_id_type=MESH)
    for d in range(1, ROW):
        peer = base + lax.rem(j + d, ROW)
        pl.semaphore_signal(barrier, inc=1, device_id={"seq": peer}, device_id_type=MESH)
    for d in range(1, ROWS):
        peer = lax.rem(y + d, ROWS) * ROW + j
        pl.semaphore_signal(barrier, inc=1, device_id={"seq": peer}, device_id_type=MESH)
    for d in range(1, LAT):
        peer = lax.rem(me + d, LAT)
        pl.semaphore_signal(barrier, inc=1, device_id={"lat": peer}, device_id_type=MESH)
    pl.semaphore_wait(barrier, 2 + ROW - 1 + ROWS - 1 + LAT - 1)

    full, own_shard = (wenc, wdec), (wenc_hbm, wdec_hbm)
    sibling = base + 2 * zh + 1 - core

    def shard_id(dy, dz):
        return lax.rem(y + dy, ROWS) * 4 + lax.rem(zh + dz, 4)

    def shard(a, s, c, half=None):
        if half is None:
            return full[a].at[s, c]
        return full[a].at[s, c, pl.ds(32 * half, 32), :]

    def slab(a, dy, c):
        return full[a].at[pl.ds(lax.rem(y + dy, ROWS) * 4, 4), c]

    def seq_at(dy, dz):
        return shard_id(dy, dz) * 2 + core

    def passed(a, s, sem, to, half=None):
        block = shard(a, s, core, half)
        return remote(block, block, sem, gr.at[a, half or 0, s], seq=to)

    def along_z(a, up):
        s, sem = shard_id(0, 0), z1s.at[a, up]
        return remote(
            own_shard[a], shard(a, s, core), sem, gr.at[a, 0, s], seq=seq_at(0, 1 if up else 3)
        )

    def along_z_on(a, half):
        s, to = (shard_id(0, 3), seq_at(0, 1)) if half == 0 else (shard_id(0, 1), seq_at(0, 3))
        return passed(a, s, z2s.at[a, half], to, half)

    def along_y(a, dz, up):
        s, to, sem = shard_id(0, dz), seq_at(1 if up else 3, 0), y1s.at[a, dz, up]
        if dz == 0:
            return remote(own_shard[a], shard(a, s, core), sem, gr.at[a, 0, s], seq=to)
        return passed(a, s, sem, to)

    def along_y_on(a, dz, half):
        s, to = (shard_id(3, dz), seq_at(1, 0)) if half == 0 else (shard_id(1, dz), seq_at(3, 0))
        return passed(a, s, y2s.at[a, dz, half], to, half)

    def across(a, dy):
        block = slab(a, dy, core)
        return remote(block, block, cs.at[a, dy], cr.at[a, dy], seq=sibling)

    def landed(a, dy, dz, half=None):
        s = shard_id(dy, dz)
        passed(a, s, cs.at[a, 0], sibling, half).wait_recv()

    def landed_across(a):
        for dy in range(ROWS):
            block = slab(a, dy, 1 - core)
            remote(block, block, cs.at[a, dy], cr.at[a, dy], seq=sibling).wait_recv()

    def start_z(a):
        for up in range(2):
            along_z(a, up).start()

    def start_y(a, dz):
        for up in range(2):
            along_y(a, dz, up).start()

    def from_z(a):
        for half, dz in enumerate((3, 1)):
            landed(a, 0, dz)
            along_z_on(a, half).start()
        start_y(a, 3)
        start_y(a, 1)

    def from_z_on(a):
        for half in range(2):
            landed(a, 0, 2, half)
        start_y(a, 2)
        loads[a].wait()
        across(a, 0).start()

    def from_y(a, dz):
        for half, dy in enumerate((3, 1)):
            landed(a, dy, dz)
            along_y_on(a, dz, half).start()
            if dz == 2:
                across(a, dy).start()

    def from_y_on(a):
        for dz in range(4):
            for half in range(2):
                landed(a, 2, dz, half)
        across(a, 2).start()

    loads = [
        pltpu.make_async_copy(wenc_hbm, shard(0, shard_id(0, 0), core), wsem.at[0]),
        pltpu.make_async_copy(wdec_hbm, shard(1, shard_id(0, 0), core), wsem.at[1]),
        pltpu.make_async_copy(wout_hbm, wout_ref, wsem.at[2]),
    ]
    halos = []
    for i, (ref, lo, width) in enumerate(((q_ref, 0, 256), (k_ref, 256, 256), (v_ref, 512, 512))):
        halos.append(
            remote(
                ref.at[pl.ds(T - 16, 16), :],
                halo.at[:, pl.ds(lo, width)],
                hs.at[i], hr.at[i], seq=right,
            )
        )
        halos[-1].start()
        pad[pl.ds(16, T), lo : lo + width] = ref[...].astype(F32)
    start_z(0)
    start_y(0, 0)
    start_y(1, 0)
    for copy in loads:
        copy.start()
    for copy in halos:
        copy.wait()
    pad[pl.ds(0, 16), :] = jnp.where(seq == 0, 0.0, halo[...].astype(F32))

    bds[0:4, :] = beta_ref[...]
    bds[4:8, :] = decay_ref[...]
    for g in range(8):
        cols = slice(g * W, (g + 1) * W)
        taps = (cq_ref, ck_ref, cv_ref)[min(g // 2, 2)]
        lo = (g - 2 * min(g // 2, 2)) * W
        total = taps[0:1, lo : lo + W] * pad[13 : 13 + T, cols]
        for tap in range(1, 4):
            total = total + taps[tap : tap + 1, lo : lo + W] * pad[13 + tap : 13 + tap + T, cols]
        total = silu(total)
        if g < 4:
            total = total * lax.rsqrt(jnp.sum(total * total, axis=1, keepdims=True) + EPSILON)
        if g < 2:
            qs[:, cols] = total * (W**-0.5)
        elif g < 4:
            ks[:, (g - 2) * W : (g - 1) * W] = total
        else:
            vs[:, (g - 4) * W : (g - 3) * W] = total

    row = lax.broadcasted_iota(jnp.int32, (C, C), 0)
    col = lax.broadcasted_iota(jnp.int32, (C, C), 1)
    lower = (col <= row).astype(F32)
    upper = (row <= col).astype(F32)
    eye = (row == col).astype(F32)
    ones = jnp.ones((C, C), F32)

    systems, scores, keys, queries, cums = [], [], [], [], []
    for c in range(T // C):
        rows = slice(c * C, (c + 1) * C)
        bd = bds[:, rows]
        beta_col = mm6(eye, 1.0 / (1.0 + jnp.exp(-bd)), ((1,), (1,)))
        cum_col = mm6(lower, bd, ((1,), (1,)))
        cum_row = mm6(bd, upper)
        cums.append((beta_col, cum_col, cum_row, mm6(bd, ones)))
        for kh in range(2):
            k = ks[rows, kh * W : (kh + 1) * W]
            q = qs[rows, kh * W : (kh + 1) * W]
            kp, qp = halves(k), halves(q)
            gram = mm3(kp, kp, ((1,), (1,)))
            score = mm3(qp, kp, ((1,), (1,)))
            keys.append(k)
            queries.append(q)
            for h in (2 * kh, 2 * kh + 1):
                spread = cum_col[:, 4 + h : 5 + h] - cum_row[4 + h : 5 + h, :]
                within = jnp.where(col <= row, jnp.exp(jnp.minimum(spread, 0.0)), 0.0)
                systems.append(
                    jnp.where(col < row, beta_col[:, h : h + 1] * gram * within, 0.0)
                )
                scores.append((score * within).astype(BF16))
    solved = [x.astype(BF16) for x in triangular_inverses(systems, row, col)]
    from_z(0)

    key_t = [k.T for k in keys]
    every = [(c, h) for c in range(T // C) for h in range(H)]
    fresh, out, new = [], [], []
    for i, (c, h) in enumerate(every):
        beta_col, cum_col, _, _ = cums[c]
        beta = beta_col[:, h : h + 1]
        growth = jnp.exp(cum_col[:, 4 + h : 5 + h])
        v = vs[c * C : (c + 1) * C, h * W : (h + 1) * W]
        k = keys[2 * c + h // 2]
        targets = jnp.concatenate([beta * v, (beta * growth) * k], axis=1)
        fresh.append(mm(solved[i], targets).astype(BF16))
    for i, (c, h) in enumerate(every):
        _, _, cum_row, tot_row = cums[c]
        remain = jnp.exp(tot_row[4 + h : 5 + h, :] - cum_row[4 + h : 5 + h, :])
        out.append(mm(scores[i], fresh[i]))
        new.append(mm(key_t[2 * c + h // 2] * remain, fresh[i]))
    from_y(0, 0)
    from_y(1, 0)
    comp, acur = [None] * H, [None] * H
    for i, (c, h) in enumerate(every):
        _, cum_col, _, tot_row = cums[c]
        rows = slice(c * C, (c + 1) * C)
        q_map = jnp.exp(cum_col[:, 4 + h : 5 + h]) * queries[2 * c + h // 2] - out[i][:, W:]
        decay = jnp.exp(tot_row[4 + h : 5 + h, :])
        if c == 0:
            ql[h, rows, :] = q_map.astype(BF16)
            ol[h, rows, :] = out[i][:, :W]
            comp[h], acur[h] = new[i], decay
            continue
        a, so_far = acur[h], comp[h]
        read = mm(q_map, so_far)
        ql[h, rows, :] = (a * q_map - read[:, W:]).astype(BF16)
        ol[h, rows, :] = out[i][:, :W] + read[:, :W]
        turned = mm(new[i][:, W:], so_far)
        comp[h] = (
            jnp.concatenate([decay, decay], axis=1) * so_far
            - turned
            + jnp.concatenate([new[i][:, :W], a * new[i][:, W:]], axis=1)
        )
        acur[h] = a * decay

    def split_row(a):
        high = a.astype(BF16).astype(F32)
        mid = (a - high).astype(BF16).astype(F32)
        low = a - high - mid
        r = lax.broadcasted_iota(jnp.int32, (16, W), 0)
        block = jnp.where(r == 0, high, jnp.where(r == 1, mid, jnp.where(r == 2, low, 0.0)))
        return jnp.concatenate([block, block], axis=1).astype(BF16)

    def joined_row(ref):
        return jnp.sum(ref[C : C + 16, :W].astype(F32), axis=0, keepdims=True)

    for h in range(H):
        msg[h, :C, :] = comp[h].astype(BF16)
        msg[h, C:, :] = split_row(acur[h])

    def to_handler(h):
        return remote(msg.at[h], slots.at[j], ms.at[h], mr.at[j], seq=base + 2 * h)

    for h in range(H):

        @pl.when(j != 2 * h)
        def _():
            to_handler(h).start()

        @pl.when(j == 2 * h)
        def _():
            slots[j] = msg[h]

    def total_to(d):
        peer = lax.rem(y + d, ROWS)
        return remote(tot, tslots.at[y], ts.at[d - 1], tr.at[y], seq=peer * ROW + j)

    def state_to(i):
        return remote(sout.at[i], sin.at[zh], ss.at[i], sr.at[zh], seq=base + i)

    @pl.when(core == 0)
    def _():
        for i in range(ROW):

            @pl.when(i != j)
            def _():
                remote(msg.at[0], slots.at[i], ms.at[0], mr.at[i], seq=base + i).wait_recv()

            maps = slots[i, :C, :]
            a_new = joined_row(slots.at[i])
            if i == 0:
                now, a_now = maps.astype(F32), a_new
            else:
                a_old, old = aprefix[i - 1, 0:1, :], prefix[i - 1]
                turned = mm(maps[:, W:], old)
                new = maps.astype(F32)
                a2 = jnp.concatenate([a_new, a_new], axis=1)
                now = (
                    a2 * old - turned + jnp.concatenate([new[:, :W], a_old * new[:, W:]], axis=1)
                )
                a_now = a_old * a_new
            prefix[i] = now
            aprefix[i] = jnp.broadcast_to(a_now, (8, W))
        tot[:C, :] = prefix[ROW - 1].astype(BF16)
        tot[C:, :] = split_row(aprefix[ROW - 1, 0:1, :])
        for d in range(1, ROWS):
            total_to(d).start()
        tslots[y] = tot[...]
        from_z_on(0)
        start_z(1)
        state = jnp.zeros((C, W), F32)
        for i in range(ROWS):

            @pl.when(i != y)
            def _():
                remote(tot, tslots.at[i], ts.at[0], tr.at[i], seq=i * ROW + j).wait_recv()

            maps = tslots[i]
            later = (
                joined_row(tslots.at[i]) * state
                - mm(maps[:C, W:], state)
                + maps[:C, :W].astype(F32)
            )
            state = jnp.where(i < y, later, state)
        for i in range(ROW):
            if i == 0:
                mine = state
            else:
                mine = (
                    aprefix[i - 1, 0:1, :] * state
                    - mm(prefix[i - 1, :, W:], state)
                    + prefix[i - 1, :, :W]
                )
            sout[i] = mine.astype(BF16)

            @pl.when(i != j)
            def _():
                state_to(i).start()

            @pl.when(i == j)
            def _():
                sin[zh] = sout[i]

    @pl.when(core == 1)
    def _():
        start_z(1)
        from_z_on(0)

    from_y(0, 3)
    from_y(0, 1)
    gated = []
    for h in range(H):

        @pl.when(j != 2 * h)
        def _():
            remote(sout.at[0], sin.at[h], ss.at[0], sr.at[h], seq=base + 2 * h).wait_recv()

    from_z(1)
    for h in range(H):
        delta = ol[h] + mm(ql[h], sin[h])
        squares = jnp.mean(delta * delta, axis=1, keepdims=True)
        gate = silu(z_ref[:, h * W : (h + 1) * W].astype(F32))
        gated.append((delta * lax.rsqrt(squares + EPSILON) * gain_ref[...] * gate).astype(BF16))
    gated = jnp.concatenate(gated, axis=1)
    loads[2].wait()

    zl, x = me // 4, lax.rem(me, 4)
    other = 1 - zl
    HALF = T // 2

    def lat_at(plane, column):
        return plane * 4 + column

    def column_at(d):
        return lax.rem(x + d, 4)

    def token_rows(block):
        return pl.ds(block * HALF, HALF)

    class ColumnsFirst:
        def __init__(self, src, rows, bufs, sems):
            self.src, self.rows = src, rows
            self.xarr, self.zsend, self.zrecv = bufs
            self.xs, self.xr, self.zs, self.zr = sems

        def to_column(self, d):
            c = column_at(d)
            return remote(
                self.src.at[:, c, self.rows, :], self.xarr.at[:, x],
                self.xs.at[d - 1], self.xr.at[x], lat=lat_at(zl, c),
            )

        def to_plane(self):
            return remote(self.zsend, self.zrecv, self.zs.at[0], self.zr.at[0], lat=lat_at(other, x))

        def turn(self):
            own = self.src[zl, x, self.rows, :].astype(F32)
            theirs = self.src[other, x, self.rows, :].astype(F32)
            for d in range(1, 4):
                c = column_at(d)
                remote(
                    self.src.at[:, c, self.rows, :], self.xarr.at[:, c],
                    self.xs.at[0], self.xr.at[c], lat=lat_at(zl, c),
                ).wait_recv()
                own = own + self.xarr[zl, c].astype(F32)
                theirs = theirs + self.xarr[other, c].astype(F32)
            self.zsend[...] = theirs.astype(BF16)
            self.to_plane().start()
            self.own = own

        def finish(self):
            self.to_plane().wait_recv()
            return self.own + self.zrecv[...].astype(F32)

        def close(self):
            for d in range(1, 4):
                self.to_column(d).wait_send()
            self.to_plane().wait_send()

    class PlanesFirst:
        def __init__(self, src, rows, bufs, sems):
            self.src, self.rows = src, rows
            self.zarr, self.xsend, self.xrecv = bufs
            self.xs, self.xr, self.zs, self.zr = sems

        def to_plane(self):
            return remote(
                self.src.at[other, :, self.rows, :], self.zarr,
                self.zs.at[0], self.zr.at[0], lat=lat_at(other, x),
            )

        def to_column(self, d):
            c = column_at(d)
            return remote(
                self.xsend.at[c], self.xrecv.at[x], self.xs.at[d - 1], self.xr.at[x],
                lat=lat_at(zl, c),
            )

        def turn(self):
            self.to_plane().wait_recv()
            for d in range(1, 4):
                c = column_at(d)
                both = self.src[zl, c, self.rows, :].astype(F32) + self.zarr[c].astype(F32)
                self.xsend[c] = both.astype(BF16)
                self.to_column(d).start()
            self.own = self.src[zl, x, self.rows, :].astype(F32) + self.zarr[x].astype(F32)

        def finish(self):
            total = self.own
            for d in range(1, 4):
                c = column_at(d)
                remote(
                    self.xsend.at[c], self.xrecv.at[c], self.xs.at[0], self.xr.at[c],
                    lat=lat_at(zl, c),
                ).wait_recv()
                total = total + self.xrecv[c].astype(F32)
            return total

        def close(self):
            for d in range(1, 4):
                self.to_column(d).wait_send()
            self.to_plane().wait_send()

    def project(block):
        rows = gated[block * HALF : (block + 1) * HALF, :]
        for lane in range(LAT):
            part[lane // 4, lane % 4, token_rows(block), :] = mm(
                rows, wout_ref[:, lane * 256 : (lane + 1) * 256]
            ).astype(BF16)

    sums1 = (
        ColumnsFirst(part, token_rows(0), (xarr1, zsend1, zrecv1), (xs1.at[0], xr1.at[0], zs1.at[0], zr1.at[0])),
        PlanesFirst(part, token_rows(1), (zarr1, xsend1, xrecv1), (xs1.at[1], xr1.at[1], zs1.at[1], zr1.at[1])),
    )
    sums2 = (
        PlanesFirst(decoded, token_rows(0), (zarr2, xsend2, xrecv2), (xs2.at[0], xr2.at[0], zs2.at[0], zr2.at[0])),
        ColumnsFirst(decoded, token_rows(1), (xarr2, zsend2, zrecv2), (xs2.at[1], xr2.at[1], zs2.at[1], zr2.at[1])),
    )

    def slot(block, plane, column):
        return streams.at[plane, column, token_rows(block), :]

    def give(block, plane, column, sem, **to):
        here = slot(block, plane, column)
        return remote(here, here, sem, gr_lat.at[block, lat_at(plane, column)], **to)

    def give_own_x(block, d):
        return give(block, zl, x, gxs.at[block, d - 1], lat=lat_at(zl, column_at(d)))

    def give_own_z(block):
        return give(block, zl, x, gzs.at[block], lat=lat_at(other, x))

    def give_on(block, d):
        if block == 0:
            return give(0, other, x, ga.at[0, d - 1], lat=lat_at(zl, column_at(d)))
        return give(1, zl, column_at(d), ga.at[1, d - 1], lat=lat_at(other, x))

    def got(block, plane, column):
        give(block, plane, column, gzs.at[block], lat=lat_at(other, x)).wait_recv()

    def enter_stream(block):
        rows = token_rows(block)
        summed = sums1[block].finish()
        streams[zl, x, rows, :] = (res_ref[rows, :].astype(F32) + summed).astype(BF16)
        for d in range(1, 4):
            give_own_x(block, d).start()
        give_own_z(block).start()

    def normalise(block):
        rows = token_rows(block)
        squares = jnp.zeros((HALF, 1), F32)
        for plane in range(2):
            for column in range(4):
                wide = streams[plane, column, rows, :].astype(F32)
                squares = squares + jnp.sum(wide * wide, axis=1, keepdims=True)
        scale = lax.rsqrt(squares * (1.0 / 2048.0) + EPSILON)
        for lane in range(LAT):
            cols = slice(lane * 256, (lane + 1) * 256)
            wide = streams[lane // 4, lane % 4, rows, :].astype(F32)
            normed[rows, cols] = (wide * scale * pgain_ref[:, cols]).astype(BF16)

    def encode(block):
        rows = token_rows(block)

        def step(i, _):
            cols = pl.ds(pl.multiple_of(i * 256, 256), 256)
            features = wenc[:, :, :, cols].reshape(2048, 256)
            pre = jnp.dot(normed[rows, :], features, preferred_element_type=F32)
            latents[rows, cols] = jnp.maximum(pre + benc_ref[:, cols], 0.0).astype(BF16)
            return 0

        lax.fori_loop(0, LAT, step, 0)

    def decode(plane, column):
        rows = wdec[pl.ds(lat_at(plane, column) * 2, 2)].reshape(256, 2048)
        decoded[plane, column] = lax.dot_general(
            latents[...], rows, (((1,), (1,)), ((), ())), preferred_element_type=F32
        ).astype(BF16)

    def leave(block):
        rows = token_rows(block)
        total = sums2[block].finish() + streams[zl, x, rows, :].astype(F32) + bdec_ref[...]
        out_ref[rows, :] = total.astype(BF16)

    project(0)
    for d in range(1, 4):
        sums1[0].to_column(d).start()
    project(1)
    sums1[1].to_plane().start()
    from_z_on(1)
    from_y(0, 2)
    sums1[0].turn()
    sums1[1].turn()
    from_y(1, 3)
    from_y(1, 1)
    enter_stream(0)
    enter_stream(1)
    from_y_on(0)
    got(0, other, x)
    for d in range(1, 4):
        give_on(0, d).start()
    for d in range(1, 4):
        got(1, zl, column_at(d))
        give_on(1, d).start()
    from_y(1, 2)
    for d in range(1, 4):
        got(0, zl, column_at(d))
    for d in range(1, 4):
        got(0, other, column_at(d))
    normalise(0)
    landed_across(0)
    encode(0)
    from_y_on(1)
    for d in range(4):
        got(1, other, column_at(d))
    normalise(1)
    encode(1)
    landed_across(1)

    def other_plane(i, _):
        decode(other, i)
        return 0

    lax.fori_loop(0, 4, other_plane, 0)
    sums2[0].to_plane().start()

    def own_plane(d, _):
        decode(zl, column_at(d))
        sums2[1].to_column(d).start()
        return 0

    lax.fori_loop(1, 4, own_plane, 0)
    decode(zl, x)

    for h in range(H):

        @pl.when(j != 2 * h)
        def _():
            to_handler(h).wait_send()

    @pl.when(core == 0)
    def _():
        for d in range(1, ROWS):
            total_to(d).wait_send()
        for i in range(ROW):

            @pl.when(i != j)
            def _():
                state_to(i).wait_send()

    for sums in sums1:
        sums.close()
    for block in range(2):
        for d in range(1, 4):
            give_own_x(block, d).wait_send()
            give_on(block, d).wait_send()
        give_own_z(block).wait_send()
    for a in range(2):
        for side in range(2):
            along_z(a, side).wait_send()
            along_z_on(a, side).wait_send()
        for dz in range(4):
            for side in range(2):
                along_y(a, dz, side).wait_send()
                along_y_on(a, dz, side).wait_send()
        for dy in range(ROWS):
            across(a, dy).wait_send()
    sums2[0].turn()
    sums2[1].turn()
    leave(0)
    leave(1)
    for sums in sums2:
        sums.close()


def layer(*args):
    vmem = pl.BlockSpec(memory_space=pltpu.VMEM)
    block = pltpu.VMEM((2, 4, T, 256), BF16)
    dma = pltpu.SemaphoreType.DMA
    return pl.pallas_call(
        layer_kernel,
        out_shape=jax.ShapeDtypeStruct((T, 256), BF16),
        in_specs=[vmem] * 14 + [pl.BlockSpec(memory_space=pl.ANY)] * 3,
        out_specs=vmem,
        scratch_shapes=[
            pltpu.VMEM((8, T), F32),
            pltpu.VMEM((16, 1024), BF16),
            pltpu.VMEM((T + 16, 1024), F32),
            pltpu.VMEM((T, 256), F32),
            pltpu.VMEM((T, 256), F32),
            pltpu.VMEM((T, 512), F32),
            pltpu.VMEM((H, T, W), BF16),
            pltpu.VMEM((H, T, W), F32),
            pltpu.VMEM((H, C + 16, 2 * W), BF16),
            pltpu.VMEM((ROW, C + 16, 2 * W), BF16),
            pltpu.VMEM((ROW, C, 2 * W), F32),
            pltpu.VMEM((ROW, 8, W), F32),
            pltpu.VMEM((C + 16, 2 * W), BF16),
            pltpu.VMEM((ROWS, C + 16, 2 * W), BF16),
            pltpu.VMEM((ROW, C, W), BF16),
            pltpu.VMEM((H, C, W), BF16),
            pltpu.VMEM((512, 2048), BF16),
            pltpu.VMEM((16, 2, 64, 2048), BF16),
            pltpu.VMEM((16, 2, 64, 2048), BF16),
            block,
            block,
            pltpu.VMEM((T, 2048), BF16),
            pltpu.VMEM((T, 2048), BF16),
            block,
        ]
        + [
            pltpu.VMEM((2, 4, T // 2, 256), BF16),
            pltpu.VMEM((T // 2, 256), BF16),
            pltpu.VMEM((T // 2, 256), BF16),
            pltpu.VMEM((4, T // 2, 256), BF16),
            pltpu.VMEM((4, T // 2, 256), BF16),
            pltpu.VMEM((4, T // 2, 256), BF16),
        ]
        * 2
        + [
            dma((3,)),
            dma((3,)),
            dma((H,)),
            dma((ROW,)),
            dma((ROWS - 1,)),
            dma((ROWS,)),
            dma((ROW,)),
            dma((H,)),
            dma((3,)),
        ]
        + [dma((2, 3)), dma((2, 4)), dma((2, 1)), dma((2, 1))] * 2
        + [dma((2, 3)), dma((2,)), dma((2, 3)), dma((2, LAT))]
        + [dma((2, 2, 16)), dma((2, 4)), dma((2, 4))]
        + [dma((2, 2)), dma((2, 2)), dma((2, 4, 2)), dma((2, 4, 2))],
        compiler_params=pltpu.CompilerParams(
            collective_id=0, has_side_effects=True, vmem_limit_bytes=VMEM_LIMIT
        ),
        name="layer",
    )(*args)


def per_device(
    q_raw,
    k_raw,
    v_raw,
    z_gate,
    beta_raw,
    decay_log,
    conv_q,
    conv_k,
    conv_v,
    norm_gain,
    w_out,
    residual,
    post_gain,
    w_enc,
    b_enc,
    w_dec,
    b_dec,
):
    return layer(
        q_raw, k_raw, v_raw, z_gate, beta_raw, decay_log, conv_q, conv_k, conv_v,
        norm_gain[None, :], residual, post_gain[None, :], b_enc[None, :], b_dec[None, :], w_out, w_enc, w_dec,
    )


def solution(mesh):
    return jax.shard_map(
        per_device,
        mesh=mesh,
        in_specs=(
            P("seq", "lat"),
            P("seq", "lat"),
            P("seq", "lat"),
            P("seq", "lat"),
            P("lat", "seq"),
            P("lat", "seq"),
            P(None, "lat"),
            P(None, "lat"),
            P(None, "lat"),
            P(),
            P("lat", None),
            P("seq", "lat"),
            P(),
            P("seq", "lat"),
            P("lat"),
            P("seq", "lat"),
            P("lat"),
        ),
        out_specs=P("seq", "lat"),
        check_vma=False,
    )
```

```python
import functools

import jax
import jax.numpy as jnp
from jax import lax
from jax.experimental import pallas as pl
from jax.experimental.pallas import tpu as pltpu
from jax.sharding import PartitionSpec as P

F32 = jnp.float32
BF16 = jnp.bfloat16
EPSILON = 1e-06
T = 384
C = 128
H = 4
W = 128
ROW = 8
ROWS = 4
LAT = 8
TOP = lax.Precision.HIGHEST
MESH = pl.DeviceIdType.MESH
VMEM_LIMIT = 56 << 20


def mm(a, b, dims=((1,), (0,))):
    return lax.dot_general(
        a.astype(BF16), b.astype(BF16), (dims, ((), ())), preferred_element_type=F32
    )


def halves(a):
    high = a.astype(BF16)
    return high, (a - high.astype(F32)).astype(BF16)


def mm3(a, b, dims=((1,), (0,))):
    ah, al = a
    bh, bl = b
    dot = lambda x, y: lax.dot_general(x, y, (dims, ((), ())), preferred_element_type=F32)
    if dims != ((1,), (0,)):
        return dot(ah, bh) + (dot(ah, bl) + dot(al, bh))
    both = dot(jnp.concatenate([ah, al], axis=1), jnp.concatenate([bh, bh], axis=0))
    return both + dot(ah, bl)


def mm6(a, b, dims=((1,), (0,))):
    return lax.dot_general(a, b, (dims, ((), ())), precision=TOP, preferred_element_type=F32)


def silu(v):
    return v / (1.0 + jnp.exp(-v))


def triangular_inverses(systems, row, col):
    first = ((row & 1) == 1) & (col == row - 1)
    eye = (row == col).astype(F32)
    solved = [eye - jnp.where(first, a, 0.0) for a in systems]
    for level in range(1, 7):
        block_row, block_col = row >> level, col >> level
        mask = ((block_row & 1) == 1) & (block_col == block_row - 1)
        size = 1 << level
        if size < 8:
            parts = [halves(x) for x in solved]
            below = [mm3(halves(jnp.where(mask, a, 0.0)), x) for a, x in zip(systems, parts)]
            solved = [x - mm3(p, halves(b)) for x, p, b in zip(solved, parts, below)]
            continue
        shape = (C // (2 * size), 2, size, C)
        odd = lambda m: m.reshape(shape)[:, 1].reshape(C // 2, C)
        parts = [halves(x) for x in solved]
        below = [mm3(halves(odd(jnp.where(mask, a, 0.0))), x) for a, x in zip(systems, parts)]
        zero = jnp.zeros((C // (2 * size), 1, size, C), F32)
        full = [
            jnp.concatenate([zero, b.reshape(zero.shape)], axis=1).reshape(C, C) for b in below
        ]
        change = [mm3(halves(odd(x)), halves(f)) for x, f in zip(solved, full)]
        solved = [
            x - jnp.concatenate([zero, c.reshape(zero.shape)], axis=1).reshape(C, C)
            for x, c in zip(solved, change)
        ]
    return solved


def remote(src, dst, send, recv, **where):
    return pltpu.make_async_remote_copy(
        src_ref=src,
        dst_ref=dst,
        send_sem=send,
        recv_sem=recv,
        device_id=where,
        device_id_type=MESH,
    )


def layer_kernel(
    q_ref, k_ref, v_ref, z_ref, beta_ref, decay_ref, cq_ref, ck_ref, cv_ref, gain_ref,
    res_ref, pgain_ref, benc_ref, bdec_ref, wout_hbm, wenc_hbm, wdec_hbm,
    out_ref,
    bds, halo, pad, qs, ks, vs, ql, ol, msg, slots, prefix, aprefix, tot, tslots, sout, sin,
    wout_ref, wenc, wdec, part, streams, normed, latents, decoded,
    xarr1, zsend1, zrecv1, zarr1, xsend1, xrecv1, xarr2, zsend2, zrecv2, zarr2, xsend2, xrecv2,
    hs, hr, ms, mr, ts, tr, ss, sr,
    wsem, xs1, xr1, zs1, zr1, xs2, xr2, zs2, zr2, gxs, gzs, ga, gr_lat,
    gr, cr, cs, z1s, z2s, y1s, y2s,
):
    seq = lax.axis_index("seq")
    me = lax.axis_index("lat")
    n_seq = ROW * ROWS
    right, left = lax.rem(seq + 1, n_seq), lax.rem(seq + n_seq - 1, n_seq)
    y, j = seq // ROW, lax.rem(seq, ROW)
    zh, core = j // 2, lax.rem(j, 2)
    base = y * ROW

    barrier = pltpu.get_barrier_semaphore()
    pl.semaphore_signal(barrier, inc=1, device_id={"seq": right}, device_id_type=MESH)
    pl.semaphore_signal(barrier, inc=1, device_id={"seq": left}, device_id_type=MESH)
    for d in range(1, ROW):
        peer = base + lax.rem(j + d, ROW)
        pl.semaphore_signal(barrier, inc=1, device_id={"seq": peer}, device_id_type=MESH)
    for d in range(1, ROWS):
        peer = lax.rem(y + d, ROWS) * ROW + j
        pl.semaphore_signal(barrier, inc=1, device_id={"seq": peer}, device_id_type=MESH)
    for d in range(1, LAT):
        peer = lax.rem(me + d, LAT)
        pl.semaphore_signal(barrier, inc=1, device_id={"lat": peer}, device_id_type=MESH)
    pl.semaphore_wait(barrier, 2 + ROW - 1 + ROWS - 1 + LAT - 1)

    full, own_shard = (wenc, wdec), (wenc_hbm, wdec_hbm)
    sibling = base + 2 * zh + 1 - core

    def shard_id(dy, dz):
        return lax.rem(y + dy, ROWS) * 4 + lax.rem(zh + dz, 4)

    def shard(a, s, c, half=None):
        if half is None:
            return full[a].at[s, c]
        return full[a].at[s, c, pl.ds(32 * half, 32), :]

    def slab(a, dy, c):
        return full[a].at[pl.ds(lax.rem(y + dy, ROWS) * 4, 4), c]

    def seq_at(dy, dz):
        return shard_id(dy, dz) * 2 + core

    def passed(a, s, sem, to, half=None):
        block = shard(a, s, core, half)
        return remote(block, block, sem, gr.at[a, half or 0, s], seq=to)

    def along_z(a, up):
        s, sem = shard_id(0, 0), z1s.at[a, up]
        return remote(
            own_shard[a], shard(a, s, core), sem, gr.at[a, 0, s], seq=seq_at(0, 1 if up else 3)
        )

    def along_z_on(a, half):
        s, to = (shard_id(0, 3), seq_at(0, 1)) if half == 0 else (shard_id(0, 1), seq_at(0, 3))
        return passed(a, s, z2s.at[a, half], to, half)

    def along_y(a, dz, up):
        s, to, sem = shard_id(0, dz), seq_at(1 if up else 3, 0), y1s.at[a, dz, up]
        if dz == 0:
            return remote(own_shard[a], shard(a, s, core), sem, gr.at[a, 0, s], seq=to)
        return passed(a, s, sem, to)

    def along_y_on(a, dz, half):
        s, to = (shard_id(3, dz), seq_at(1, 0)) if half == 0 else (shard_id(1, dz), seq_at(3, 0))
        return passed(a, s, y2s.at[a, dz, half], to, half)

    def across(a, dy):
        block = slab(a, dy, core)
        return remote(block, block, cs.at[a, dy], cr.at[a, dy], seq=sibling)

    def landed(a, dy, dz, half=None):
        s = shard_id(dy, dz)
        passed(a, s, cs.at[a, 0], sibling, half).wait_recv()

    def landed_across(a):
        for dy in range(ROWS):
            block = slab(a, dy, 1 - core)
            remote(block, block, cs.at[a, dy], cr.at[a, dy], seq=sibling).wait_recv()

    def start_z(a):
        for up in range(2):
            along_z(a, up).start()

    def start_y(a, dz):
        for up in range(2):
            along_y(a, dz, up).start()

    def from_z(a):
        for half, dz in enumerate((3, 1)):
            landed(a, 0, dz)
            along_z_on(a, half).start()
        start_y(a, 3)
        start_y(a, 1)

    def from_z_on(a):
        for half in range(2):
            landed(a, 0, 2, half)
        start_y(a, 2)
        loads[a].wait()
        across(a, 0).start()

    def from_y(a, dz):
        for half, dy in enumerate((3, 1)):
            landed(a, dy, dz)
            along_y_on(a, dz, half).start()
            if dz == 2:
                across(a, dy).start()

    def from_y_on(a):
        for dz in range(4):
            for half in range(2):
                landed(a, 2, dz, half)
        across(a, 2).start()

    loads = [
        pltpu.make_async_copy(wenc_hbm, shard(0, shard_id(0, 0), core), wsem.at[0]),
        pltpu.make_async_copy(wdec_hbm, shard(1, shard_id(0, 0), core), wsem.at[1]),
        pltpu.make_async_copy(wout_hbm, wout_ref, wsem.at[2]),
    ]
    halos = []
    for i, (ref, lo, width) in enumerate(((q_ref, 0, 256), (k_ref, 256, 256), (v_ref, 512, 512))):
        halos.append(
            remote(
                ref.at[pl.ds(T - 16, 16), :],
                halo.at[:, pl.ds(lo, width)],
                hs.at[i], hr.at[i], seq=right,
            )
        )
        halos[-1].start()
        pad[pl.ds(16, T), lo : lo + width] = ref[...].astype(F32)
    start_z(0)
    start_y(0, 0)
    start_y(1, 0)
    for copy in loads:
        copy.start()
    for copy in halos:
        copy.wait()
    pad[pl.ds(0, 16), :] = jnp.where(seq == 0, 0.0, halo[...].astype(F32))

    bds[0:4, :] = beta_ref[...]
    bds[4:8, :] = decay_ref[...]
    for g in range(8):
        cols = slice(g * W, (g + 1) * W)
        taps = (cq_ref, ck_ref, cv_ref)[min(g // 2, 2)]
        lo = (g - 2 * min(g // 2, 2)) * W
        total = taps[0:1, lo : lo + W] * pad[13 : 13 + T, cols]
        for tap in range(1, 4):
            total = total + taps[tap : tap + 1, lo : lo + W] * pad[13 + tap : 13 + tap + T, cols]
        total = silu(total)
        if g < 4:
            total = total * lax.rsqrt(jnp.sum(total * total, axis=1, keepdims=True) + EPSILON)
        if g < 2:
            qs[:, cols] = total * (W**-0.5)
        elif g < 4:
            ks[:, (g - 2) * W : (g - 1) * W] = total
        else:
            vs[:, (g - 4) * W : (g - 3) * W] = total

    row = lax.broadcasted_iota(jnp.int32, (C, C), 0)
    col = lax.broadcasted_iota(jnp.int32, (C, C), 1)
    lower = (col <= row).astype(F32)
    upper = (row <= col).astype(F32)
    eye = (row == col).astype(F32)
    ones = jnp.ones((C, C), F32)

    systems, scores, keys, queries, cums = [], [], [], [], []
    for c in range(T // C):
        rows = slice(c * C, (c + 1) * C)
        bd = bds[:, rows]
        beta_col = mm6(eye, 1.0 / (1.0 + jnp.exp(-bd)), ((1,), (1,)))
        cum_col = mm6(lower, bd, ((1,), (1,)))
        cum_row = mm6(bd, upper)
        cums.append((beta_col, cum_col, cum_row, mm6(bd, ones)))
        for kh in range(2):
            k = ks[rows, kh * W : (kh + 1) * W]
            q = qs[rows, kh * W : (kh + 1) * W]
            kp, qp = halves(k), halves(q)
            gram = mm3(kp, kp, ((1,), (1,)))
            score = mm3(qp, kp, ((1,), (1,)))
            keys.append(k)
            queries.append(q)
            for h in (2 * kh, 2 * kh + 1):
                spread = cum_col[:, 4 + h : 5 + h] - cum_row[4 + h : 5 + h, :]
                within = jnp.where(col <= row, jnp.exp(jnp.minimum(spread, 0.0)), 0.0)
                systems.append(
                    jnp.where(col < row, beta_col[:, h : h + 1] * gram * within, 0.0)
                )
                scores.append((score * within).astype(BF16))
    solved = [x.astype(BF16) for x in triangular_inverses(systems, row, col)]
    from_z(0)

    key_t = [k.T for k in keys]
    every = [(c, h) for c in range(T // C) for h in range(H)]
    fresh, out, new = [], [], []
    for i, (c, h) in enumerate(every):
        beta_col, cum_col, _, _ = cums[c]
        beta = beta_col[:, h : h + 1]
        growth = jnp.exp(cum_col[:, 4 + h : 5 + h])
        v = vs[c * C : (c + 1) * C, h * W : (h + 1) * W]
        k = keys[2 * c + h // 2]
        targets = jnp.concatenate([beta * v, (beta * growth) * k], axis=1)
        fresh.append(mm(solved[i], targets).astype(BF16))
    for i, (c, h) in enumerate(every):
        _, _, cum_row, tot_row = cums[c]
        remain = jnp.exp(tot_row[4 + h : 5 + h, :] - cum_row[4 + h : 5 + h, :])
        out.append(mm(scores[i], fresh[i]))
        new.append(mm(key_t[2 * c + h // 2] * remain, fresh[i]))
    from_y(0, 0)
    from_y(1, 0)
    comp, acur = [None] * H, [None] * H
    for i, (c, h) in enumerate(every):
        _, cum_col, _, tot_row = cums[c]
        rows = slice(c * C, (c + 1) * C)
        q_map = jnp.exp(cum_col[:, 4 + h : 5 + h]) * queries[2 * c + h // 2] - out[i][:, W:]
        decay = jnp.exp(tot_row[4 + h : 5 + h, :])
        if c == 0:
            ql[h, rows, :] = q_map.astype(BF16)
            ol[h, rows, :] = out[i][:, :W]
            comp[h], acur[h] = new[i], decay
            continue
        a, so_far = acur[h], comp[h]
        read = mm(q_map, so_far)
        ql[h, rows, :] = (a * q_map - read[:, W:]).astype(BF16)
        ol[h, rows, :] = out[i][:, :W] + read[:, :W]
        turned = mm(new[i][:, W:], so_far)
        comp[h] = (
            jnp.concatenate([decay, decay], axis=1) * so_far
            - turned
            + jnp.concatenate([new[i][:, :W], a * new[i][:, W:]], axis=1)
        )
        acur[h] = a * decay

    def split_row(a):
        high = a.astype(BF16).astype(F32)
        mid = (a - high).astype(BF16).astype(F32)
        low = a - high - mid
        r = lax.broadcasted_iota(jnp.int32, (16, W), 0)
        block = jnp.where(r == 0, high, jnp.where(r == 1, mid, jnp.where(r == 2, low, 0.0)))
        return jnp.concatenate([block, block], axis=1).astype(BF16)

    def joined_row(ref):
        return jnp.sum(ref[C : C + 16, :W].astype(F32), axis=0, keepdims=True)

    for h in range(H):
        msg[h, :C, :] = comp[h].astype(BF16)
        msg[h, C:, :] = split_row(acur[h])

    def to_handler(h):
        return remote(msg.at[h], slots.at[j], ms.at[h], mr.at[j], seq=base + 2 * h)

    for h in range(H):

        @pl.when(j != 2 * h)
        def _():
            to_handler(h).start()

        @pl.when(j == 2 * h)
        def _():
            slots[j] = msg[h]

    def total_to(d):
        peer = lax.rem(y + d, ROWS)
        return remote(tot, tslots.at[y], ts.at[d - 1], tr.at[y], seq=peer * ROW + j)

    def state_to(i):
        return remote(sout.at[i], sin.at[zh], ss.at[i], sr.at[zh], seq=base + i)

    @pl.when(core == 0)
    def _():
        for i in range(ROW):

            @pl.when(i != j)
            def _():
                remote(msg.at[0], slots.at[i], ms.at[0], mr.at[i], seq=base + i).wait_recv()

            maps = slots[i, :C, :]
            a_new = joined_row(slots.at[i])
            if i == 0:
                now, a_now = maps.astype(F32), a_new
            else:
                a_old, old = aprefix[i - 1, 0:1, :], prefix[i - 1]
                turned = mm(maps[:, W:], old)
                new = maps.astype(F32)
                a2 = jnp.concatenate([a_new, a_new], axis=1)
                now = (
                    a2 * old - turned + jnp.concatenate([new[:, :W], a_old * new[:, W:]], axis=1)
                )
                a_now = a_old * a_new
            prefix[i] = now
            aprefix[i] = jnp.broadcast_to(a_now, (8, W))
        tot[:C, :] = prefix[ROW - 1].astype(BF16)
        tot[C:, :] = split_row(aprefix[ROW - 1, 0:1, :])
        for d in range(1, ROWS):
            total_to(d).start()
        tslots[y] = tot[...]
        from_z_on(0)
        start_z(1)
        state = jnp.zeros((C, W), F32)
        for i in range(ROWS):

            @pl.when(i != y)
            def _():
                remote(tot, tslots.at[i], ts.at[0], tr.at[i], seq=i * ROW + j).wait_recv()

            maps = tslots[i]
            later = (
                joined_row(tslots.at[i]) * state
                - mm(maps[:C, W:], state)
                + maps[:C, :W].astype(F32)
            )
            state = jnp.where(i < y, later, state)
        for i in range(ROW):
            if i == 0:
                mine = state
            else:
                mine = (
                    aprefix[i - 1, 0:1, :] * state
                    - mm(prefix[i - 1, :, W:], state)
                    + prefix[i - 1, :, :W]
                )
            sout[i] = mine.astype(BF16)

            @pl.when(i != j)
            def _():
                state_to(i).start()

            @pl.when(i == j)
            def _():
                sin[zh] = sout[i]

    @pl.when(core == 1)
    def _():
        start_z(1)
        from_z_on(0)

    from_y(0, 3)
    from_y(0, 1)
    from_z(1)
    gated = []
    for h in range(H):

        @pl.when(j != 2 * h)
        def _():
            remote(sout.at[0], sin.at[h], ss.at[0], sr.at[h], seq=base + 2 * h).wait_recv()

    for h in range(H):
        delta = ol[h] + mm(ql[h], sin[h])
        squares = jnp.mean(delta * delta, axis=1, keepdims=True)
        gate = silu(z_ref[:, h * W : (h + 1) * W].astype(F32))
        gated.append((delta * lax.rsqrt(squares + EPSILON) * gain_ref[...] * gate).astype(BF16))
    gated = jnp.concatenate(gated, axis=1)
    loads[2].wait()

    zl, x = me // 4, lax.rem(me, 4)
    other = 1 - zl
    HALF = T // 2

    def lat_at(plane, column):
        return plane * 4 + column

    def column_at(d):
        return lax.rem(x + d, 4)

    def token_rows(block):
        return pl.ds(block * HALF, HALF)

    class ColumnsFirst:
        def __init__(self, src, rows, bufs, sems):
            self.src, self.rows = src, rows
            self.xarr, self.zsend, self.zrecv = bufs
            self.xs, self.xr, self.zs, self.zr = sems

        def to_column(self, d):
            c = column_at(d)
            return remote(
                self.src.at[:, c, self.rows, :], self.xarr.at[:, x],
                self.xs.at[d - 1], self.xr.at[x], lat=lat_at(zl, c),
            )

        def to_plane(self):
            return remote(self.zsend, self.zrecv, self.zs.at[0], self.zr.at[0], lat=lat_at(other, x))

        def turn(self):
            own = self.src[zl, x, self.rows, :].astype(F32)
            theirs = self.src[other, x, self.rows, :].astype(F32)
            for d in range(1, 4):
                c = column_at(d)
                remote(
                    self.src.at[:, c, self.rows, :], self.xarr.at[:, c],
                    self.xs.at[0], self.xr.at[c], lat=lat_at(zl, c),
                ).wait_recv()
                own = own + self.xarr[zl, c].astype(F32)
                theirs = theirs + self.xarr[other, c].astype(F32)
            self.zsend[...] = theirs.astype(BF16)
            self.to_plane().start()
            self.own = own

        def finish(self):
            self.to_plane().wait_recv()
            return self.own + self.zrecv[...].astype(F32)

        def close(self):
            for d in range(1, 4):
                self.to_column(d).wait_send()
            self.to_plane().wait_send()

    class PlanesFirst:
        def __init__(self, src, rows, bufs, sems):
            self.src, self.rows = src, rows
            self.zarr, self.xsend, self.xrecv = bufs
            self.xs, self.xr, self.zs, self.zr = sems

        def to_plane(self):
            return remote(
                self.src.at[other, :, self.rows, :], self.zarr,
                self.zs.at[0], self.zr.at[0], lat=lat_at(other, x),
            )

        def to_column(self, d):
            c = column_at(d)
            return remote(
                self.xsend.at[c], self.xrecv.at[x], self.xs.at[d - 1], self.xr.at[x],
                lat=lat_at(zl, c),
            )

        def turn(self):
            self.to_plane().wait_recv()
            for d in range(1, 4):
                c = column_at(d)
                both = self.src[zl, c, self.rows, :].astype(F32) + self.zarr[c].astype(F32)
                self.xsend[c] = both.astype(BF16)
                self.to_column(d).start()
            self.own = self.src[zl, x, self.rows, :].astype(F32) + self.zarr[x].astype(F32)

        def finish(self):
            total = self.own
            for d in range(1, 4):
                c = column_at(d)
                remote(
                    self.xsend.at[c], self.xrecv.at[c], self.xs.at[0], self.xr.at[c],
                    lat=lat_at(zl, c),
                ).wait_recv()
                total = total + self.xrecv[c].astype(F32)
            return total

        def close(self):
            for d in range(1, 4):
                self.to_column(d).wait_send()
            self.to_plane().wait_send()

    def project(block):
        rows = gated[block * HALF : (block + 1) * HALF, :]
        for lane in range(LAT):
            part[lane // 4, lane % 4, token_rows(block), :] = mm(
                rows, wout_ref[:, lane * 256 : (lane + 1) * 256]
            ).astype(BF16)

    sums1 = (
        ColumnsFirst(part, token_rows(0), (xarr1, zsend1, zrecv1), (xs1.at[0], xr1.at[0], zs1.at[0], zr1.at[0])),
        PlanesFirst(part, token_rows(1), (zarr1, xsend1, xrecv1), (xs1.at[1], xr1.at[1], zs1.at[1], zr1.at[1])),
    )
    sums2 = (
        PlanesFirst(decoded, token_rows(0), (zarr2, xsend2, xrecv2), (xs2.at[0], xr2.at[0], zs2.at[0], zr2.at[0])),
        ColumnsFirst(decoded, token_rows(1), (xarr2, zsend2, zrecv2), (xs2.at[1], xr2.at[1], zs2.at[1], zr2.at[1])),
    )

    def slot(block, plane, column):
        return streams.at[plane, column, token_rows(block), :]

    def give(block, plane, column, sem, **to):
        here = slot(block, plane, column)
        return remote(here, here, sem, gr_lat.at[block, lat_at(plane, column)], **to)

    def give_own_x(block, d):
        return give(block, zl, x, gxs.at[block, d - 1], lat=lat_at(zl, column_at(d)))

    def give_own_z(block):
        return give(block, zl, x, gzs.at[block], lat=lat_at(other, x))

    def give_on(block, d):
        if block == 0:
            return give(0, other, x, ga.at[0, d - 1], lat=lat_at(zl, column_at(d)))
        return give(1, zl, column_at(d), ga.at[1, d - 1], lat=lat_at(other, x))

    def got(block, plane, column):
        give(block, plane, column, gzs.at[block], lat=lat_at(other, x)).wait_recv()

    def enter_stream(block):
        rows = token_rows(block)
        summed = sums1[block].finish()
        streams[zl, x, rows, :] = (res_ref[rows, :].astype(F32) + summed).astype(BF16)
        for d in range(1, 4):
            give_own_x(block, d).start()
        give_own_z(block).start()

    def normalise(block):
        rows = token_rows(block)
        squares = jnp.zeros((HALF, 1), F32)
        for plane in range(2):
            for column in range(4):
                wide = streams[plane, column, rows, :].astype(F32)
                squares = squares + jnp.sum(wide * wide, axis=1, keepdims=True)
        scale = lax.rsqrt(squares * (1.0 / 2048.0) + EPSILON)
        for lane in range(LAT):
            cols = slice(lane * 256, (lane + 1) * 256)
            wide = streams[lane // 4, lane % 4, rows, :].astype(F32)
            normed[rows, cols] = (wide * scale * pgain_ref[:, cols]).astype(BF16)

    def encode(block):
        rows = token_rows(block)

        def step(i, _):
            cols = pl.ds(pl.multiple_of(i * 256, 256), 256)
            features = wenc[:, :, :, cols].reshape(2048, 256)
            pre = jnp.dot(normed[rows, :], features, preferred_element_type=F32)
            latents[rows, cols] = jnp.maximum(pre + benc_ref[:, cols], 0.0).astype(BF16)
            return 0

        lax.fori_loop(0, LAT, step, 0)

    def decode(plane, column):
        rows = wdec[pl.ds(lat_at(plane, column) * 2, 2)].reshape(256, 2048)
        decoded[plane, column] = lax.dot_general(
            latents[...], rows, (((1,), (1,)), ((), ())), preferred_element_type=F32
        ).astype(BF16)

    def leave(block):
        rows = token_rows(block)
        total = sums2[block].finish() + streams[zl, x, rows, :].astype(F32) + bdec_ref[...]
        out_ref[rows, :] = total.astype(BF16)

    project(0)
    for d in range(1, 4):
        sums1[0].to_column(d).start()
    project(1)
    sums1[1].to_plane().start()
    from_z_on(1)
    from_y(0, 2)
    sums1[0].turn()
    sums1[1].turn()
    from_y(1, 3)
    from_y(1, 1)
    enter_stream(0)
    enter_stream(1)
    from_y_on(0)
    got(0, other, x)
    for d in range(1, 4):
        give_on(0, d).start()
    for d in range(1, 4):
        got(1, zl, column_at(d))
        give_on(1, d).start()
    from_y(1, 2)
    for d in range(1, 4):
        got(0, zl, column_at(d))
    for d in range(1, 4):
        got(0, other, column_at(d))
    normalise(0)
    landed_across(0)
    encode(0)
    from_y_on(1)
    for d in range(4):
        got(1, other, column_at(d))
    normalise(1)
    encode(1)
    landed_across(1)

    def other_plane(i, _):
        decode(other, i)
        return 0

    lax.fori_loop(0, 4, other_plane, 0)
    sums2[0].to_plane().start()

    def own_plane(d, _):
        decode(zl, column_at(d))
        sums2[1].to_column(d).start()
        return 0

    lax.fori_loop(1, 4, own_plane, 0)
    decode(zl, x)

    for h in range(H):

        @pl.when(j != 2 * h)
        def _():
            to_handler(h).wait_send()

    @pl.when(core == 0)
    def _():
        for d in range(1, ROWS):
            total_to(d).wait_send()
        for i in range(ROW):

            @pl.when(i != j)
            def _():
                state_to(i).wait_send()

    for sums in sums1:
        sums.close()
    for block in range(2):
        for d in range(1, 4):
            give_own_x(block, d).wait_send()
            give_on(block, d).wait_send()
        give_own_z(block).wait_send()
    for a in range(2):
        for side in range(2):
            along_z(a, side).wait_send()
            along_z_on(a, side).wait_send()
        for dz in range(4):
            for side in range(2):
                along_y(a, dz, side).wait_send()
                along_y_on(a, dz, side).wait_send()
        for dy in range(ROWS):
            across(a, dy).wait_send()
    sums2[0].turn()
    sums2[1].turn()
    leave(0)
    leave(1)
    for sums in sums2:
        sums.close()


def layer(*args):
    vmem = pl.BlockSpec(memory_space=pltpu.VMEM)
    block = pltpu.VMEM((2, 4, T, 256), BF16)
    dma = pltpu.SemaphoreType.DMA
    return pl.pallas_call(
        layer_kernel,
        out_shape=jax.ShapeDtypeStruct((T, 256), BF16),
        in_specs=[vmem] * 14 + [pl.BlockSpec(memory_space=pl.ANY)] * 3,
        out_specs=vmem,
        scratch_shapes=[
            pltpu.VMEM((8, T), F32),
            pltpu.VMEM((16, 1024), BF16),
            pltpu.VMEM((T + 16, 1024), F32),
            pltpu.VMEM((T, 256), F32),
            pltpu.VMEM((T, 256), F32),
            pltpu.VMEM((T, 512), F32),
            pltpu.VMEM((H, T, W), BF16),
            pltpu.VMEM((H, T, W), F32),
            pltpu.VMEM((H, C + 16, 2 * W), BF16),
            pltpu.VMEM((ROW, C + 16, 2 * W), BF16),
            pltpu.VMEM((ROW, C, 2 * W), F32),
            pltpu.VMEM((ROW, 8, W), F32),
            pltpu.VMEM((C + 16, 2 * W), BF16),
            pltpu.VMEM((ROWS, C + 16, 2 * W), BF16),
            pltpu.VMEM((ROW, C, W), BF16),
            pltpu.VMEM((H, C, W), BF16),
            pltpu.VMEM((512, 2048), BF16),
            pltpu.VMEM((16, 2, 64, 2048), BF16),
            pltpu.VMEM((16, 2, 64, 2048), BF16),
            block,
            block,
            pltpu.VMEM((T, 2048), BF16),
            pltpu.VMEM((T, 2048), BF16),
            block,
        ]
        + [
            pltpu.VMEM((2, 4, T // 2, 256), BF16),
            pltpu.VMEM((T // 2, 256), BF16),
            pltpu.VMEM((T // 2, 256), BF16),
            pltpu.VMEM((4, T // 2, 256), BF16),
            pltpu.VMEM((4, T // 2, 256), BF16),
            pltpu.VMEM((4, T // 2, 256), BF16),
        ]
        * 2
        + [
            dma((3,)),
            dma((3,)),
            dma((H,)),
            dma((ROW,)),
            dma((ROWS - 1,)),
            dma((ROWS,)),
            dma((ROW,)),
            dma((H,)),
            dma((3,)),
        ]
        + [dma((2, 3)), dma((2, 4)), dma((2, 1)), dma((2, 1))] * 2
        + [dma((2, 3)), dma((2,)), dma((2, 3)), dma((2, LAT))]
        + [dma((2, 2, 16)), dma((2, 4)), dma((2, 4))]
        + [dma((2, 2)), dma((2, 2)), dma((2, 4, 2)), dma((2, 4, 2))],
        compiler_params=pltpu.CompilerParams(
            collective_id=0, has_side_effects=True, vmem_limit_bytes=VMEM_LIMIT
        ),
        name="layer",
    )(*args)


def per_device(
    q_raw,
    k_raw,
    v_raw,
    z_gate,
    beta_raw,
    decay_log,
    conv_q,
    conv_k,
    conv_v,
    norm_gain,
    w_out,
    residual,
    post_gain,
    w_enc,
    b_enc,
    w_dec,
    b_dec,
):
    return layer(
        q_raw, k_raw, v_raw, z_gate, beta_raw, decay_log, conv_q, conv_k, conv_v,
        norm_gain[None, :], residual, post_gain[None, :], b_enc[None, :], b_dec[None, :], w_out, w_enc, w_dec,
    )


def solution(mesh):
    return jax.shard_map(
        per_device,
        mesh=mesh,
        in_specs=(
            P("seq", "lat"),
            P("seq", "lat"),
            P("seq", "lat"),
            P("seq", "lat"),
            P("lat", "seq"),
            P("lat", "seq"),
            P(None, "lat"),
            P(None, "lat"),
            P(None, "lat"),
            P(),
            P("lat", None),
            P("seq", "lat"),
            P(),
            P("seq", "lat"),
            P("lat"),
            P("seq", "lat"),
            P("lat"),
        ),
        out_specs=P("seq", "lat"),
        check_vma=False,
    )
```
